256 devices in a mesh: phase: 4 (over x), dp: 16 (over z, core), fsdp: 4 (over y).
Axes of the slice: x: 4, y: 4, z: 8, core: 2. Of those that a mesh axis runs over, the one named last changes fastest.
Arguments:
- audio_frames: bfloat16 [16384, 1280], P(('dp', 'fsdp')), may hold values from -6 to 6
- vision_patches: bfloat16 [16384, 1280], P(('dp', 'fsdp')), may hold values from -6 to 6
- audio_blocks: int32 [64, 256], P(('dp', 'fsdp')), may hold values from 0 to 7, never falling along the last dimension, each value on 1 to 128 neighbouring positions
- vision_windows: int32 [64, 256], P(('dp', 'fsdp')), may hold values from 0 to 7, never falling along the last dimension, each value on 1 to 112 neighbouring positions
- insert_order: int32 [64, 768], P(('dp', 'fsdp')), may hold values from 0 to 767, each once within a row
- text_embeds: bfloat16 [49152, 8192], P(('dp', 'fsdp'), 'phase'), may hold values from -6 to 6
- ln_gain: bfloat16 [4, 1280], P('phase'), may hold values from 0.5 to 1.5
- attn_qkv: bfloat16 [4, 1280, 3840], P('phase', ('dp', 'fsdp')), may hold values from -1 to 1
- attn_out: bfloat16 [4, 1280, 1280], P('phase', ('dp', 'fsdp')), may hold values from -0.15625 to 0.15625
- projector: bfloat16 [1280, 8192], P(('dp', 'fsdp'), 'phase'), may hold values from -0.15625 to 0.15625
Outputs:
- llm_rows: bfloat16 [49152, 8192], P(('dp', 'fsdp'), 'phase')
The draws below stay inside these ranges and needn't reach their ends.
Inputs may be any that keep to these rules, and one draw needn't show every extreme that they name: `audio_blocks`: each row never falls, each block holds 1 to 128 frames, one exactly 128. `vision_windows`: each row never falls, each window holds 1 to 112 patches, one exactly 112. `insert_order`: each row is a permutation of 0 to 767.
All inputs are finite; a program needn't handle non-finite values.
Results may differ from the reference program's by a relative error of at most 0.012.
The reference program's roundings to bfloat16 on the way count: a program that leaves them out, or rounds other values in their place, can miss the bound.
Values may be sent and summed in bfloat16 or wider, within the bound.
A program may use at most 192 MiB of HBM per device.

```python
import math
import jax
import jax.numpy as jnp
import numpy as np
from jax import lax

D = 1280
E = 8192
R_DEV = 256
TOK_DEV = 768
SEQS = 64
N_PHASE = 4
N_DP = 16
N_FSDP = 4


def draw_audio_frames(key, part):
    key = jax.random.fold_in(key, 3)
    rows = jnp.clip(jax.random.normal(key, (SEQS * R_DEV, D), jnp.float32), -6.0, 6.0)
    return rows.astype(jnp.bfloat16)


def draw_vision_patches(key, part):
    key = jax.random.fold_in(key, 5)
    rows = jnp.clip(jax.random.normal(key, (SEQS * R_DEV, D), jnp.float32), -6.0, 6.0)
    return rows.astype(jnp.bfloat16)


def draw_attn_qkv(key, part):
    key = jax.random.fold_in(key, 7)
    base = jnp.clip(jax.random.normal(key, (N_PHASE, D, 3 * D), jnp.float32), -6.0, 6.0) * D ** (-0.5)
    return base.astype(jnp.bfloat16)


def block_levels(key, dims, pieces, smallest, top_value):
    factor_of, own = 1.0, jax.random.fold_in(key, 6)
    for axis_at, blocks in pieces:
        steps = jnp.exp(jax.random.uniform(jax.random.fold_in(own, axis_at), (blocks,), jnp.float32, smallest / len(pieces), top_value / len(pieces)))
        factor_of = factor_of * jnp.repeat(steps, dims[axis_at] // blocks).reshape([-1 if axis == axis_at else 1 for axis in range(len(dims))])
    return factor_of


def profile(number_of, total, reach, skew):
    loads = [(1 << 20) // math.isqrt(grade ** skew) + 1 for grade in range(2, number_of + 1)]
    spare, counts = total - reach - (number_of - 1), [1] * (number_of - 1)
    while spare > 0:
        candidates = [i for i in range(number_of - 1) if counts[i] < reach]
        pool, budget = sum([loads[i] for i in candidates]), spare
        for i in candidates:
            addition = min(reach - counts[i], max(1, budget * loads[i] // pool), spare)
            counts[i] = counts[i] + addition
            spare = spare - addition
    return np.array([reach] + counts)


def ragged(stream_key, number_of, total, bound, slope):
    if number_of == 2:
        one = jax.random.randint(stream_key, (), max(1, total - bound), min(bound, total - 1) + 1)
        return jnp.stack([one, total - one])
    lengths = jnp.asarray(profile(number_of, total, bound, slope), jnp.int32)
    pairs = (number_of - 1) // 2
    giver, sink = lengths[1:1 + 2 * pairs:2], lengths[2:2 + 2 * pairs:2]
    room = jnp.minimum(giver - 1, bound - sink)
    shifted = jax.random.randint(jax.random.fold_in(stream_key, 1), (pairs,), 0, 1 << 20) % (room + 1)
    lengths = lengths.at[1:1 + 2 * pairs:2].set(giver - shifted).at[2:2 + 2 * pairs:2].set(sink + shifted)
    return lengths[jax.random.permutation(jax.random.fold_in(stream_key, 2), number_of)]


def centred(rng, dims, scale, reach, cuts=(), kind=jnp.bfloat16):
    factor_of = block_levels(rng, dims, cuts, -0.22, 0.18) if cuts else 1.0
    array = jax.random.normal(rng, dims, jnp.float32) * scale * factor_of
    return jnp.minimum(jnp.maximum(array, -reach), reach).astype(kind)


def setup_inputs(seed: int = 0) -> dict:
    streams_of = jax.random.split(jax.random.key(seed), 11)
    return {
        "audio_frames": draw_audio_frames(jax.random.fold_in(streams_of[10], 71), 0),
        "vision_patches": draw_vision_patches(jax.random.fold_in(streams_of[10], 71), 0),
        "audio_blocks": jax.vmap(lambda own: jnp.searchsorted(jnp.cumsum(ragged(own, R_DEV // 32, R_DEV, 128, 1)), jnp.arange(R_DEV), side="right"))(jax.random.split(streams_of[2], SEQS)).reshape((SEQS, R_DEV)).astype(jnp.int32),
        "vision_windows": jax.vmap(lambda own: jnp.searchsorted(jnp.cumsum(ragged(own, R_DEV // 32, R_DEV, 112, 1)), jnp.arange(R_DEV), side="right"))(jax.random.split(streams_of[3], SEQS)).reshape((SEQS, R_DEV)).astype(jnp.int32),
        "insert_order": jax.vmap(lambda own: jax.random.permutation(own, TOK_DEV))(jax.random.split(streams_of[4], SEQS)).reshape((SEQS, TOK_DEV)).astype(jnp.int32),
        "text_embeds": centred(streams_of[5], (SEQS * TOK_DEV, E), 1.0, 6.0, ((0, 64), (1, 4))),
        "ln_gain": jnp.clip(1.0 + 0.1 * jax.random.normal(streams_of[6], (N_PHASE, D), jnp.float32), 0.5, 1.5).astype(jnp.bfloat16),
        "attn_qkv": draw_attn_qkv(jax.random.fold_in(streams_of[10], 71), 0),
        "attn_out": centred(streams_of[8], (N_PHASE, D, D), D ** -0.5, 0.15625, ((0, 4), (1, 64))),
        "projector": centred(streams_of[9], (D, E), D ** -0.5, 0.15625, ((0, 64), (1, 4))),
    }


def norm_rows(input_rows, gain_vec):
    values = input_rows.astype(jnp.float32)
    centre = values - lax.optimization_barrier(jnp.mean(values, axis=-1, keepdims=True))
    spread = lax.optimization_barrier(jnp.mean(centre * centre, axis=-1, keepdims=True))
    return (centre * lax.rsqrt(spread + 1e-05) * gain_vec.astype(jnp.float32)).astype(jnp.bfloat16)

def attention_core(query, keys, values, ids_query, ids_keys, head_count):
    row_count, model_width = query.shape
    head_size = model_width // head_count
    query_heads = query.reshape(row_count, head_count, head_size).astype(jnp.float32)
    key_heads = keys.reshape(-1, head_count, head_size).astype(jnp.float32)
    value_heads = values.reshape(-1, head_count, head_size).astype(jnp.float32)
    scores = jnp.einsum('qhd,khd->hqk', query_heads, key_heads) * head_size ** (-0.5)
    same_block = ids_query[:, None] == ids_keys[None, :]
    scores = jnp.where(same_block[None], scores, -1e+30)
    row_max = lax.optimization_barrier(jnp.max(scores, axis=-1, keepdims=True))
    exponent = jnp.exp(scores - row_max)
    weights = (exponent / lax.optimization_barrier(jnp.sum(exponent, axis=-1, keepdims=True))).astype(jnp.bfloat16)
    mixed_rows = jnp.einsum('hqk,khd->qhd', weights.astype(jnp.float32), value_heads)
    return mixed_rows.reshape(row_count, model_width).astype(jnp.bfloat16)

def encoder_layer(input_rows, block_ids, w_qkv, w_out, gain_vec, head_count):
    model_width = input_rows.shape[1]
    normed = norm_rows(input_rows, gain_vec)
    packed = jnp.dot(normed, w_qkv, preferred_element_type=jnp.float32).astype(jnp.bfloat16)
    mixed_rows = attention_core(packed[:, :model_width], packed[:, model_width:2 * model_width], packed[:, 2 * model_width:], block_ids, block_ids, head_count)
    update = jnp.dot(mixed_rows, w_out, preferred_element_type=jnp.float32)
    return (input_rows.astype(jnp.float32) + update).astype(jnp.bfloat16)

def reference(audio_frames, vision_patches, audio_blocks, vision_windows, insert_order, text_embeds, ln_gain, attn_qkv, attn_out, projector):
    groups = N_DP * N_FSDP
    model_width = audio_frames.shape[1]
    audio_parts = audio_frames.reshape(groups, R_DEV, model_width)
    vision_parts = vision_patches.reshape(groups, R_DEV, model_width)
    text_parts = text_embeds.reshape(groups, TOK_DEV, E)

    def encode(members):
        audio_part, audio_ids, vision_part, vision_ids, text_part, order_row = members
        audio_part = encoder_layer(audio_part, audio_ids, attn_qkv[0], attn_out[0], ln_gain[0], model_width // 64)
        audio_part = encoder_layer(audio_part, audio_ids, attn_qkv[1], attn_out[1], ln_gain[1], model_width // 64)
        vision_part = encoder_layer(vision_part, vision_ids, attn_qkv[2], attn_out[2], ln_gain[2], model_width // 80)
        vision_part = encoder_layer(vision_part, vision_ids, attn_qkv[3], attn_out[3], ln_gain[3], model_width // 80)
        encoded = jnp.concatenate([audio_part, vision_part], axis=0)
        projected = jnp.dot(encoded, projector, preferred_element_type=jnp.float32).astype(jnp.bfloat16)
        return text_part.at[order_row[:2 * R_DEV]].set(projected)
    placed = lax.map(encode, (audio_parts, audio_blocks, vision_parts, vision_windows, text_parts, insert_order))
    return placed.reshape(groups * TOK_DEV, E)
```

```python
import jax
import jax.numpy as jnp
from jax import lax
from jax.experimental import pallas as pl
from jax.experimental.pallas import tpu as pltpu
from jax.sharding import PartitionSpec as P

MESH = pl.DeviceIdType.MESH
BF = jnp.bfloat16
F32 = jnp.float32
ROWS = 256
HALF = 640
N_COPIES = 300


class Copies:
    def __init__(self, send, recv):
        self.send, self.recv, self.made = send, recv, []

    def start(self, src, dst, to):
        at = len(self.made)
        copy = pltpu.make_async_remote_copy(
            src_ref=src,
            dst_ref=dst,
            send_sem=self.send.at[at],
            recv_sem=self.recv.at[at],
            device_id=to,
            device_id_type=MESH,
        )
        copy.start()
        self.made.append(copy)
        return copy

    def finish(self):
        for copy in self.made:
            if copy is not None:
                copy.wait_send()

    def wait(self, copy):
        copy.wait()
        self.made = [None if other is copy else other for other in self.made]


class Place:
    def __init__(self):
        self.p = lax.axis_index("phase")
        self.d = lax.axis_index("dp")
        self.y = lax.axis_index("fsdp")
        self.z = self.d // 2
        self.c = self.d % 2

    def z_at(self, k):
        return (self.z + (k + 8)) % 8

    def y_at(self, k):
        return (self.y + (k + 4)) % 4

    def along_z(self, k):
        return (self.p, self.z_at(k) * 2 + self.c, self.y)

    def along_y(self, k):
        return (self.p, self.d, self.y_at(k))

    def along_x(self, k):
        return ((self.p + (k + 4)) % 4, self.d, self.y)

    def twin(self):
        return (self.p, self.z * 2 + (1 - self.c), self.y)

    def partner(self):
        return (self.p + 1 - 2 * (self.p % 2), self.d, self.y)

    def slab(self, k, y, count=None):
        zz = self.z_at(k)
        at = (zz // 4) * 40 + (zz % 4) * 8 + self.c * 4
        return at + y

    def quad(self, k):
        zz = self.z_at(k)
        return (zz // 4) * 40 + (zz % 4) * 8 + self.c * 4

    def left(self, k):
        zz = self.z_at(k)
        return (zz // 4) * 40 + 32 + (zz % 4) * 2 + self.c


class Gather:
    def __init__(self, here, copies, buf, small, width, cut):
        self.h, self.cp, self.buf, self.small = here, copies, buf, small
        self.width, self.cut = width, cut
        tiles = cut // 128
        self.mid = (tiles + 1) // 2 * 128
        self.c = {}

    def reg_p(self, k, y, part=None):
        lo, hi = {None: (0, self.cut), "a": (0, self.mid), "b": (self.mid, self.cut)}[part]
        return self.buf.at[self.h.slab(k, y), :, pl.ds(lo, hi - lo)]

    def reg_q(self, y, part=None):
        mid = self.cut + (self.width - self.cut + 128) // 256 * 128
        lo, hi = {None: (self.cut, self.width), "a": (self.cut, mid), "b": (mid, self.width)}[part]
        return self.buf.at[self.h.slab(0, y), :, pl.ds(lo, hi - lo)]

    def reg_s(self, y, part=None):
        w = self.width // 4
        mid = w // 256 * 128
        lo, hi = {None: (0, w), "a": (0, mid), "b": (mid, w)}[part]
        return self.small.at[y, :, pl.ds(lo, hi - lo)]

    def reg_quad(self, k, part=None):
        lo, n = {None: (0, 4), "a": (0, 2), "b": (2, 2)}[part]
        return self.buf.at[pl.ds(self.h.quad(k) + lo, n), :, pl.ds(self.cut, self.width - self.cut)]

    def reg_left(self, k, part=None):
        half = self.width // 2
        lo, n = {None: (0, self.width), "a": (0, half), "b": (half, half)}[part]
        return self.buf.at[self.h.left(k), :, pl.ds(lo, n)]

    def go(self, name, region, to):
        self.c[name] = self.cp.start(region, region, to)

    def got(self, name):
        self.c[name].wait_recv()

    def p_send_y(self, k):
        h = self.h
        self.go(("py+", k), self.reg_p(k, h.y), h.along_y(1))
        self.go(("py-", k), self.reg_p(k, h.y), h.along_y(-1))

    def p_forward_y(self, k):
        h = self.h
        self.got(("py+", k))
        self.go(("pyy+", k), self.reg_p(k, h.y_at(-1), "a"), h.along_y(1))
        self.got(("py-", k))
        self.go(("pyy-", k), self.reg_p(k, h.y_at(1), "b"), h.along_y(-1))

    def p_end_y(self, k):
        self.got(("pyy+", k))
        self.got(("pyy-", k))

    def p_send_z(self, k):
        h = self.h
        a, b = (None, None) if k < 3 else ("a", "b")
        self.go(("pz+", k), self.reg_p(-k, h.y, a), h.along_z(1))
        self.go(("pz-", k), self.reg_p(k, h.y, b), h.along_z(-1))

    def q_send_y(self):
        h = self.h
        for tag, reg in (("s", self.reg_s), ("q", self.reg_q)):
            self.go((tag, "y+"), reg(h.y), h.along_y(1))
            self.go((tag, "y-"), reg(h.y), h.along_y(-1))

    def q_forward_y(self):
        h = self.h
        for tag, reg in (("s", self.reg_s), ("q", self.reg_q)):
            self.got((tag, "y+"))
            self.go((tag, "yy+"), reg(h.y_at(-1), "a"), h.along_y(1))
            self.got((tag, "y-"))
            self.go((tag, "yy-"), reg(h.y_at(1), "b"), h.along_y(-1))

    def q_end_y(self):
        self.got(("q", "yy+"))
        self.got(("q", "yy-"))
        self.q_send_z(0, "quad")
        self.got(("s", "yy+"))
        self.got(("s", "yy-"))
        w = self.width // 4
        parts = self.small[...].astype(F32)
        own = self.h.left(0)
        for j in range(4):
            rows = jnp.concatenate([parts[i, 4 * j : 4 * j + 4, :] for i in range(4)], axis=0)
            self.buf[own, :, j * w : (j + 1) * w] = rows.astype(BF)
        self.q_send_z(0, "left")

    def q_send_z(self, k, what):
        h = self.h
        reg = self.reg_quad if what == "quad" else self.reg_left
        a, b = (None, None) if k < 3 else ("a", "b")
        self.go((what, "z+", k), reg(-k, a), h.along_z(1))
        self.go((what, "z-", k), reg(k, b), h.along_z(-1))

    def q_forward_z(self, k):
        for what in ("quad", "left"):
            self.got((what, "z+", k))
            self.got((what, "z-", k))
            if k < 3:
                self.q_send_z(k + 1, what)

    def to_twin(self, k):
        h = self.h
        reg = self.buf.at[pl.ds(h.quad(k), 4)]
        self.go(("t", k), reg, h.twin())
        reg = self.buf.at[h.left(k)]
        self.go(("tl", k), reg, h.twin())

    def round(self, r):
        if r == 0:
            self.q_send_y()
            self.p_send_z(0)
            self.p_send_y(0)
        if r == 1:
            self.q_forward_y()
            self.got(("pz+", 0))
            self.got(("pz-", 0))
            self.p_send_z(1)
            self.p_forward_y(0)
            self.p_send_y(-1)
            self.p_send_y(1)
        if r == 2:
            self.q_end_y()
            self.got(("pz+", 1))
            self.got(("pz-", 1))
            self.p_send_z(2)
            self.p_forward_y(-1)
            self.p_forward_y(1)
            self.p_send_y(-2)
            self.p_send_y(2)
        if r == 3:
            self.got(("pz+", 2))
            self.got(("pz-", 2))
            self.p_send_z(3)
            self.q_forward_z(0)
            self.p_end_y(0)
            self.to_twin(0)
            self.p_forward_y(-2)
            self.p_forward_y(2)
            self.p_send_y(-3)
            self.p_send_y(3)
        if r == 4:
            self.got(("pz+", 3))
            self.got(("pz-", 3))
            self.p_send_y(4)
            self.q_forward_z(1)
            self.p_end_y(-1)
            self.p_end_y(1)
            self.to_twin(-1)
            self.to_twin(1)
            self.p_forward_y(-3)
            self.p_forward_y(3)
        if r == 5:
            self.q_forward_z(2)
            self.p_end_y(-2)
            self.p_end_y(2)
            self.to_twin(-2)
            self.to_twin(2)
            self.p_forward_y(4)
        if r == 6:
            self.p_end_y(-3)
            self.p_end_y(3)
            self.to_twin(-3)
            self.to_twin(3)
            self.p_end_y(4)
            self.q_forward_z(3)
            self.to_twin(4)
        if r == 7:
            for k in (0, -1, 1, -2, 2, -3, 3, 4):
                self.got(("t", k))
                self.got(("tl", k))


def flat(slabs):
    return slabs.reshape(slabs.shape[0] * slabs.shape[1], slabs.shape[2])


def dot(a, b):
    return jnp.dot(a, b, preferred_element_type=F32)


def kernel(
    audio_ref, vision_ref, ids_a_ref, ids_v_ref, order_ref, text_ref, gain_ref, qkv_ref, out_w_ref, proj_ref,
    result_ref,
    w, wp, small, small_p, send_main, send_left, raw_gains, gains,
    x_nat, x_half, xp, bias, perm, normed, packed, macc, mixed, enc, place, prj, text, out_buf,
    send_sem, recv_sem, local_sem,
):
    here = Place()
    h = here.p % 2
    side = here.p // 2
    copies = Copies(send_sem, recv_sem)

    barrier = pltpu.get_barrier_semaphore()
    greet = [here.along_z(1), here.along_z(-1), here.along_y(1), here.along_y(-1), here.along_x(1), here.along_x(-1), here.twin()]
    for to in greet:
        pl.semaphore_signal(barrier, inc=1, device_id=to, device_id_type=MESH)

    @pl.when(side == 0)
    def _():
        pltpu.make_async_copy(audio_ref, x_nat, local_sem.at[0]).start()

    @pl.when(side == 1)
    def _():
        pltpu.make_async_copy(vision_ref, x_nat, local_sem.at[0]).start()

    text_copy = pltpu.make_async_copy(text_ref, text, local_sem.at[1])
    text_copy.start()

    own = here.slab(0, here.y)
    pieces = [(qkv_ref, 0), (qkv_ref, 1280), (qkv_ref, 2560), (out_w_ref, 0)]

    def main_of(i, half):
        ref, base = pieces[i]
        at = pl.multiple_of(base + half * HALF, 128)
        return ref[0, pl.ds(0, 16), pl.ds(at, HALF)]

    def left_of(half):
        rows = []
        for ref, base in pieces:
            at = pl.multiple_of(base + half * HALF, 128)
            rows.append(ref[0, pl.ds(16, 4), pl.ds(at, HALF)].astype(F32))
        return jnp.concatenate(rows, axis=0).astype(BF)

    for i in range(4):
        send_main[:, i * HALF : (i + 1) * HALF] = main_of(i, 1 - h)
    send_left[...] = left_of(1 - h)
    raw_gains[h] = jnp.broadcast_to(gain_ref[...], (16, 1280))

    pl.semaphore_wait(barrier, len(greet))
    x_main = copies.start(send_main, w.at[h, own], here.partner())
    x_left = copies.start(send_left, small.at[h, here.y], here.partner())
    x_gain = copies.start(raw_gains.at[h], raw_gains.at[h], here.partner())

    wp[own] = proj_ref[pl.ds(0, 16), :]
    tail = proj_ref[pl.ds(16, 4), :].astype(F32)
    small_p[here.y] = jnp.concatenate([tail[:, j * 512 : (j + 1) * 512] for j in range(4)], axis=0).astype(BF)
    for i in range(4):
        w[h, own, :, i * HALF : (i + 1) * HALF] = main_of(i, h)
    small[h, here.y] = left_of(h)

    g0 = Gather(here, copies, w.at[0], small.at[0], 2560, 1920)
    g1 = Gather(here, copies, w.at[1], small.at[1], 2560, 1920)
    gp = Gather(here, copies, wp, small_p, 2048, 1536)

    x_main.wait_recv()
    x_left.wait_recv()
    x_gain.wait_recv()
    g0.round(0)

    t = lax.broadcasted_iota(jnp.int32, (1, HALF), 1)
    u = t - 512
    source = jnp.where(t < 512, (t // 16) * 20 + t % 16, (u // 4) * 20 + 16 + u % 4)
    perm[...] = (lax.broadcasted_iota(jnp.int32, (HALF, HALF), 0) == source).astype(F32).astype(BF)

    g0.round(1)
    for b in range(2):
        sl = slice(b * HALF, (b + 1) * HALF)
        for l in range(2):
            gains[l, :, sl] = dot(raw_gains[l, :, sl], perm[...]).astype(BF)

    ids = jnp.where(side == 0, ids_a_ref[...], ids_v_ref[...])
    hot = (lax.broadcasted_iota(jnp.int32, (16, ROWS), 0) == ids).astype(F32).astype(BF)
    same = lax.dot_general(hot, hot, (((0,), (0,)), ((), ())), preferred_element_type=F32)
    bias[...] = (same - 1.0) * 1e30

    @pl.when(side == 0)
    def _():
        pltpu.make_async_copy(audio_ref, x_nat, local_sem.at[0]).wait()

    @pl.when(side == 1)
    def _():
        pltpu.make_async_copy(vision_ref, x_nat, local_sem.at[0]).wait()

    g0.round(2)
    x_half[...] = x_nat[:, pl.ds(pl.multiple_of(h * HALF, 128), HALF)]
    for b in range(2):
        sl = slice(b * HALF, (b + 1) * HALF)
        xp[b] = dot(x_nat[:, sl], perm[...]).astype(BF)
    place[...] = (lax.broadcasted_iota(jnp.int32, (768, 512), 0) == order_ref[:, :512]).astype(F32).astype(BF)

    def norm(l):
        def body(i, carry):
            at = pl.ds(pl.multiple_of(i * 32, 32), 32)
            a = xp[0, at, :].astype(F32)
            b = xp[1, at, :].astype(F32)
            mean = (jnp.sum(a, axis=-1, keepdims=True) + jnp.sum(b, axis=-1, keepdims=True)) * (1.0 / 1280)
            a = a - mean
            b = b - mean
            var = (jnp.sum(a * a, axis=-1, keepdims=True) + jnp.sum(b * b, axis=-1, keepdims=True)) * (1.0 / 1280)
            scale = lax.rsqrt(var + 1e-05)
            gain = gains[l, pl.ds(0, 16), :].astype(F32)[0:1]
            normed[at, pl.ds(0, HALF)] = (a * scale * gain[:, :HALF]).astype(BF)
            normed[at, pl.ds(HALF, HALF)] = (b * scale * gain[:, HALF:]).astype(BF)
            return carry

        lax.fori_loop(0, ROWS // 32, body, 0)

    def project(l, i):
        sl = slice(i * HALF, (i + 1) * HALF)
        packed[:, sl] = dot(normed[...], flat(w[l, :, :, sl])).astype(BF)

    def head(q, k, v, keep, scale):
        s = lax.dot_general(q, jnp.where(keep, k, 0), (((1,), (1,)), ((), ())), preferred_element_type=F32)
        s = s * scale + bias[...]
        e = jnp.exp(s - jnp.max(s, axis=-1, keepdims=True))
        weights = (e / jnp.sum(e, axis=-1, keepdims=True)).astype(BF)
        return dot(weights, jnp.where(keep, v, 0))

    def attend():
        @pl.when(side == 0)
        def _():
            def body(j, carry):
                q, k, v = [packed[:, pl.ds(pl.multiple_of(i * HALF + j * 128, 128), 128)] for i in range(3)]
                lane = lax.broadcasted_iota(jnp.int32, (ROWS, 128), 1)
                total = head(q, k, v, lane < 64, 0.125) + head(q, k, v, lane >= 64, 0.125)
                macc[:, pl.ds(pl.multiple_of(j * 128, 128), 128)] = total
                return carry

            lax.fori_loop(0, 5, body, 0)

        @pl.when(side == 1)
        def _():
            macc[...] = jnp.zeros((ROWS, HALF), F32)
            for i in range(8):
                lo, hi = (80 * i) // 128 * 128, (80 * i + 80 + 127) // 128 * 128
                q, k, v = [packed[:, j * HALF + lo : j * HALF + hi] for j in range(3)]
                lane = lax.broadcasted_iota(jnp.int32, (ROWS, hi - lo), 1) + lo
                keep = (lane >= 80 * i) & (lane < 80 * i + 80)
                macc[:, lo:hi] = macc[:, lo:hi] + head(q, k, v, keep, 80 ** (-0.5))

    def out_layer(l):
        update = dot(mixed[0], flat(w[l, pl.ds(0, 40), :, pl.ds(3 * HALF, HALF)]))
        update = update + dot(mixed[1], flat(w[l, pl.ds(40, 40), :, pl.ds(3 * HALF, HALF)]))
        x_half[...] = (x_half[...].astype(F32) + update).astype(BF)

    g0.round(3)
    g1.round(0)
    g0.round(4)
    g1.round(1)
    g0.round(5)
    norm(0)
    g1.round(2)
    g0.round(6)
    g1.round(3)
    gp.round(0)
    g0.round(7)

    for i in range(3):
        project(0, i)
    g1.round(4)
    gp.round(1)
    attend()
    mixed[h] = dot(macc[...].astype(BF), perm[...]).astype(BF)
    cm0 = copies.start(mixed.at[h], mixed.at[h], here.partner())
    g1.round(5)
    gp.round(2)
    copies.wait(cm0)
    out_layer(0)
    xp[h] = dot(x_half[...], perm[...]).astype(BF)
    cx0 = copies.start(xp.at[h], xp.at[h], here.partner())
    g1.round(6)
    gp.round(3)
    g1.round(7)
    copies.wait(cx0)
    norm(1)
    for i in range(3):
        project(1, i)
    gp.round(4)
    attend()
    mixed[h] = dot(macc[...].astype(BF), perm[...]).astype(BF)
    cm1 = copies.start(mixed.at[h], mixed.at[h], here.partner())
    gp.round(5)
    copies.wait(cm1)
    out_layer(1)
    enc[here.p] = dot(x_half[...], perm[...]).astype(BF)
    up = copies.start(enc.at[here.p], enc.at[here.p], here.along_x(1))
    down = copies.start(enc.at[here.p], enc.at[here.p], here.along_x(-1))
    gp.round(6)
    up.wait_recv()
    lo = enc.at[(here.p + 3) % 4, pl.ds(0, 128)]
    up2 = copies.start(lo, lo, here.along_x(1))
    down.wait_recv()
    hi = enc.at[(here.p + 1) % 4, pl.ds(128, 128)]
    down2 = copies.start(hi, hi, here.along_x(-1))
    gp.round(7)
    text_copy.wait()
    up2.wait_recv()
    down2.wait_recv()

    def last(j, carry):
        cols = pl.ds(pl.multiple_of(j * 512, 512), 512)
        top = flat(wp[pl.ds(0, 40), :, cols])
        low = flat(wp[pl.ds(40, 40), :, cols])
        for i in range(2):
            rows = dot(enc[2 * i], top) + dot(enc[2 * i + 1], low)
            prj[pl.ds(i * ROWS, ROWS), cols] = rows.astype(BF)
        spread = dot(place[...], prj[:, cols])
        taken = jnp.sum(place[...].astype(F32), axis=-1, keepdims=True)
        out_buf[:, cols] = jnp.where(taken > 0.5, spread, text[:, cols].astype(F32)).astype(BF)
        pltpu.make_async_copy(out_buf.at[:, cols], result_ref.at[:, cols], local_sem.at[2 + j]).start()
        return carry

    lax.fori_loop(0, 4, last, 0)
    copies.finish()
    for j in range(4):
        cols = pl.ds(j * 512, 512)
        pltpu.make_async_copy(out_buf.at[:, cols], result_ref.at[:, cols], local_sem.at[2 + j]).wait()


def per_device(audio, vision, ids_a, ids_v, order, text, gain, qkv, out_w, proj):
    vm = pl.BlockSpec(memory_space=pltpu.VMEM)
    anywhere = pl.BlockSpec(memory_space=pl.ANY)
    return pl.pallas_call(
        kernel,
        out_shape=jax.ShapeDtypeStruct((768, 2048), BF),
        in_specs=[anywhere, anywhere, vm, vm, vm, anywhere, vm, vm, vm, vm],
        out_specs=anywhere,
        scratch_shapes=[
            pltpu.VMEM((2, 80, 16, 2560), BF),
            pltpu.VMEM((80, 16, 2048), BF),
            pltpu.VMEM((2, 4, 16, 640), BF),
            pltpu.VMEM((4, 16, 512), BF),
            pltpu.VMEM((16, 2560), BF),
            pltpu.VMEM((16, 640), BF),
            pltpu.VMEM((2, 16, 1280), BF),
            pltpu.VMEM((2, 16, 1280), BF),
            pltpu.VMEM((ROWS, 1280), BF),
            pltpu.VMEM((ROWS, HALF), BF),
            pltpu.VMEM((2, ROWS, HALF), BF),
            pltpu.VMEM((ROWS, ROWS), F32),
            pltpu.VMEM((HALF, HALF), BF),
            pltpu.VMEM((ROWS, 1280), BF),
            pltpu.VMEM((ROWS, 3 * HALF), BF),
            pltpu.VMEM((ROWS, HALF), F32),
            pltpu.VMEM((2, ROWS, HALF), BF),
            pltpu.VMEM((4, ROWS, HALF), BF),
            pltpu.VMEM((768, 512), BF),
            pltpu.VMEM((512, 2048), BF),
            pltpu.VMEM((768, 2048), BF),
            pltpu.VMEM((768, 2048), BF),
            pltpu.SemaphoreType.DMA((N_COPIES,)),
            pltpu.SemaphoreType.DMA((N_COPIES,)),
            pltpu.SemaphoreType.DMA((8,)),
        ],
        name="encode",
        compiler_params=pltpu.CompilerParams(collective_id=0, has_side_effects=True, vmem_limit_bytes=56 * 2**20),
        cost_estimate=pl.CostEstimate(flops=12_000_000_000, bytes_accessed=30_000_000, transcendentals=2_000_000),
    )(audio, vision, ids_a, ids_v, order, text, gain, qkv, out_w, proj)


def solution(mesh):
    placed = (
        P(("dp", "fsdp"), None),
        P(("dp", "fsdp"), None),
        P(("dp", "fsdp"), None),
        P(("dp", "fsdp"), None),
        P(("dp", "fsdp"), None),
        P(("dp", "fsdp"), "phase"),
        P("phase", None),
        P("phase", ("dp", "fsdp"), None),
        P("phase", ("dp", "fsdp"), None),
        P(("dp", "fsdp"), "phase"),
    )
    return jax.shard_map(
        per_device,
        mesh=mesh,
        in_specs=placed,
        out_specs=P(("dp", "fsdp"), "phase"),
        check_vma=False,
    )
```

```python
import jax
import jax.numpy as jnp
from jax import lax
from jax.experimental import pallas as pl
from jax.experimental.pallas import tpu as pltpu
from jax.sharding import PartitionSpec as P

MESH = pl.DeviceIdType.MESH
BF = jnp.bfloat16
F32 = jnp.float32
ROWS = 256
HALF = 640
N_SEND = 52
N_RECV = 180
CHUNK = 128


class Copies:
    def __init__(self, send, recv):
        self.send, self.recv = send, recv
        self.at, self.groups, self.sent = [0, 0], {}, []

    def sem(self, kind, name):
        if (kind, name) not in self.groups:
            self.groups[kind, name] = self.at[kind]
            self.at[kind] += 1
        return (self.send, self.recv)[kind].at[self.groups[kind, name]]

    def start(self, src, dst, to, send=None, recv=None):
        alone = send is None
        if alone:
            send = recv = ("alone", len(self.sent))
        copy = pltpu.make_async_remote_copy(
            src_ref=src,
            dst_ref=dst,
            send_sem=self.sem(0, send),
            recv_sem=self.sem(1, recv),
            device_id=to,
            device_id_type=MESH,
        )
        copy.start()
        if alone:
            self.sent.append(copy)
        return copy

    def wait(self, kind, name, size, to):
        copy = pltpu.make_async_remote_copy(
            src_ref=size,
            dst_ref=size,
            send_sem=self.sem(0, name) if kind == 0 else self.send.at[0],
            recv_sem=self.sem(1, name) if kind == 1 else self.recv.at[0],
            device_id=to,
            device_id_type=MESH,
        )
        if kind == 0:
            copy.wait_send()
        else:
            copy.wait_recv()

    def finish(self):
        for copy in self.sent:
            copy.wait_send()


class Place:
    def __init__(self):
        self.p = lax.axis_index("phase")
        self.d = lax.axis_index("dp")
        self.y = lax.axis_index("fsdp")
        self.z = self.d // 2
        self.c = self.d % 2

    def z_at(self, k):
        return (self.z + (k + 8)) % 8

    def y_at(self, k):
        return (self.y + (k + 4)) % 4

    def along_z(self, k):
        return (self.p, self.z_at(k) * 2 + self.c, self.y)

    def along_y(self, k):
        return (self.p, self.d, self.y_at(k))

    def along_x(self, k):
        return ((self.p + (k + 4)) % 4, self.d, self.y)

    def twin(self):
        return (self.p, self.z * 2 + (1 - self.c), self.y)

    def partner(self):
        return self.along_x(1 - 2 * (self.p % 2))

    def across(self):
        return self.along_x(2 * (self.p % 2) - 1)

    def slab(self, k, y, count=None):
        zz = self.z_at(k)
        at = (zz // 4) * 40 + (zz % 4) * 8 + self.c * 4
        return at + y

    def quad(self, k):
        zz = self.z_at(k)
        return (zz // 4) * 40 + (zz % 4) * 8 + self.c * 4

    def left(self, k):
        zz = self.z_at(k)
        return (zz // 4) * 40 + 32 + (zz % 4) * 2 + self.c


class Gather:
    def __init__(self, tag, here, copies, buf, small, cut):
        self.tag = tag
        self.h, self.cp, self.buf, self.small = here, copies, buf, small
        self.width, self.cut = buf.shape[2], cut
        self.short = small.shape[2]
        tiles = cut // 128
        self.mid = (tiles + 1) // 2 * 128

    def reg_p(self, k, y, part=None):
        lo, hi = {None: (0, self.cut), "a": (0, self.mid), "b": (self.mid, self.cut)}[part]
        return self.buf.at[self.h.slab(k, y), :, pl.ds(lo, hi - lo)]

    def reg_q(self, y, part=None):
        mid = self.cut + (self.width - self.cut + 128) // 256 * 128
        lo, hi = {None: (self.cut, self.width), "a": (self.cut, mid), "b": (mid, self.width)}[part]
        return self.buf.at[self.h.slab(0, y), :, pl.ds(lo, hi - lo)]

    def reg_s(self, y, part=None):
        w = self.short
        mid = w // 256 * 128
        lo, hi = {None: (0, w), "a": (0, mid), "b": (mid, w)}[part]
        return self.small.at[y, :, pl.ds(lo, hi - lo)]

    def reg_quad(self, k, part=None):
        lo, n = {None: (0, 4), "a": (0, 2), "b": (2, 2)}[part]
        return self.buf.at[pl.ds(self.h.quad(k) + lo, n), :, pl.ds(self.cut, self.width - self.cut)]

    def reg_left(self, k, part=None):
        half = self.width // 256 * 128
        lo, n = {None: (0, self.width), "a": (0, half), "b": (half, self.width - half)}[part]
        return self.buf.at[self.h.left(k), :, pl.ds(lo, n)]

    def go(self, kind, group, region, to):
        self.cp.start(region, region, to, (self.tag, kind), (self.tag, kind, group))

    def size(self, kind, n):
        if kind[0] == "p":
            return self.buf.at[pl.ds(0, n), :, pl.ds(0, self.cut)]
        if kind == "quad":
            return self.buf.at[pl.ds(0, 4 * n), :, pl.ds(self.cut, self.width - self.cut)]
        if kind == "q":
            return self.buf.at[pl.ds(0, n), :, pl.ds(self.cut, self.width - self.cut)]
        if kind == "s":
            return self.small.at[pl.ds(0, n)]
        return self.buf.at[pl.ds(0, n)]

    def got(self, kind, group, n):
        self.cp.wait(1, (self.tag, kind, group), self.size(kind, n), self.h.twin())

    def finish(self):
        for kind, n in (("pz", 7), ("py", 24), ("quad", 7), ("left", 7), ("s", 3), ("q", 3), ("t", 40)):
            self.cp.wait(0, (self.tag, kind), self.size(kind, n), self.h.twin())

    def p_send_y(self, k):
        h = self.h
        self.go("py", k, self.reg_p(k, h.y), h.along_y(1))
        self.go("py", k, self.reg_p(k, h.y), h.along_y(-1))

    def p_forward_y(self, k):
        h = self.h
        self.got("py", k, 2)
        self.go("py", ("far", k), self.reg_p(k, h.y_at(-1), "a"), h.along_y(1))
        self.go("py", ("far", k), self.reg_p(k, h.y_at(1), "b"), h.along_y(-1))

    def p_end_y(self, k):
        self.got("py", ("far", k), 1)

    def p_send_z(self, k):
        h = self.h
        a, b = (None, None) if k < 3 else ("a", "b")
        self.go("pz", k, self.reg_p(-k, h.y, a), h.along_z(1))
        self.go("pz", k, self.reg_p(k, h.y, b), h.along_z(-1))

    def p_got_z(self, k):
        self.got("pz", k, 2 if k < 3 else 1)

    def q_send_y(self):
        h = self.h
        for tag, reg in (("s", self.reg_s), ("q", self.reg_q)):
            self.go(tag, 0, reg(h.y), h.along_y(1))
            self.go(tag, 0, reg(h.y), h.along_y(-1))

    def q_forward_y(self):
        h = self.h
        for tag, reg in (("s", self.reg_s), ("q", self.reg_q)):
            self.got(tag, 0, 2)
            self.go(tag, 1, reg(h.y_at(-1), "a"), h.along_y(1))
            self.go(tag, 1, reg(h.y_at(1), "b"), h.along_y(-1))

    def q_end_y(self):
        self.got("q", 1, 1)
        self.q_send_z(0, "quad")
        self.got("s", 1, 1)
        self.gather_left()
        self.q_send_z(0, "left")

    def gather_left(self):
        parts = self.small[...].astype(F32)
        own = self.h.left(0)
        for j in range(4):
            lo, hi = j * self.short, min((j + 1) * self.short, self.width)
            rows = jnp.concatenate([parts[i, 4 * j : 4 * j + 4, : hi - lo] for i in range(4)], axis=0)
            self.buf[own, :, lo:hi] = rows.astype(BF)

    def q_send_z(self, k, what):
        h = self.h
        reg = self.reg_quad if what == "quad" else self.reg_left
        a, b = (None, None) if k < 3 else ("a", "b")
        self.go(what, k, reg(-k, a), h.along_z(1))
        self.go(what, k, reg(k, b), h.along_z(-1))

    def q_forward_z(self, k):
        for what in ("quad", "left"):
            self.got(what, k, 2 if k < 3 else 1)
            if k < 3:
                self.q_send_z(k + 1, what)

    def to_twin(self, k):
        h = self.h
        self.go("t", 0, self.buf.at[pl.ds(h.quad(k), 4)], h.twin())
        self.go("t", 0, self.buf.at[h.left(k)], h.twin())

    def round(self, r):
        if r == 0:
            self.q_send_y()
            self.p_send_z(0)
            self.p_send_y(0)
        if r == 1:
            self.p_got_z(0)
            self.p_send_z(1)
            self.q_forward_y()
            self.p_send_y(-1)
            self.p_send_y(1)
            self.p_forward_y(0)
        if r == 2:
            self.q_end_y()
            self.p_got_z(1)
            self.p_send_z(2)
            self.p_send_y(-2)
            self.p_send_y(2)
            self.p_forward_y(-1)
            self.p_forward_y(1)
        if r == 3:
            self.p_got_z(2)
            self.p_send_z(3)
            self.q_forward_z(0)
            self.p_send_y(-3)
            self.p_send_y(3)
            self.p_forward_y(-2)
            self.p_forward_y(2)
            self.p_end_y(0)
            self.to_twin(0)
        if r == 4:
            self.p_got_z(3)
            self.p_send_y(4)
            self.q_forward_z(1)
            self.p_forward_y(-3)
            self.p_forward_y(3)
            self.p_end_y(-1)
            self.p_end_y(1)
            self.to_twin(-1)
            self.to_twin(1)
        if r == 5:
            self.q_forward_z(2)
            self.p_forward_y(4)
            self.p_end_y(-2)
            self.p_end_y(2)
            self.to_twin(-2)
            self.to_twin(2)
        if r == 6:
            self.q_forward_z(3)
            self.p_end_y(-3)
            self.p_end_y(3)
            self.to_twin(-3)
            self.to_twin(3)
            self.p_end_y(4)
            self.to_twin(4)
        if r == 7:
            self.got("t", 0, 40)


def flat(slabs):
    return slabs.reshape(slabs.shape[0] * slabs.shape[1], slabs.shape[2])


def dot(a, b):
    return jnp.dot(a, b, preferred_element_type=F32)


def compact(rows, short):
    rows = rows.astype(F32)
    fill = 4 * short - rows.shape[1]
    if fill:
        rows = jnp.concatenate([rows, jnp.zeros((4, fill), F32)], axis=1)
    return jnp.concatenate([rows[:, j * short : (j + 1) * short] for j in range(4)], axis=0).astype(BF)


def kernel(
    audio_ref, vision_ref, ids_a_ref, ids_v_ref, order_ref, text_ref, gain_ref, qkv_ref, out_w_ref, proj_ref,
    result_ref,
    wq, wo, wp, small_q, small_o, small_p, send_q, send_sq, raw_gains, gains,
    x_nat, xp, bias, perm, normed, packed, macc, mixed, enc, place, text, out_buf,
    send_sem, recv_sem, local_sem,
):
    here = Place()
    h = here.p % 2
    side = here.p // 2
    copies = Copies(send_sem, recv_sem)

    barrier = pltpu.get_barrier_semaphore()
    greet = [here.along_z(1), here.along_z(-1), here.along_y(1), here.along_y(-1), here.along_x(1), here.along_x(-1), here.twin()]
    for to in greet:
        pl.semaphore_signal(barrier, inc=1, device_id=to, device_id_type=MESH)

    @pl.when(side == 0)
    def _():
        pltpu.make_async_copy(audio_ref, x_nat, local_sem.at[0]).start()

    @pl.when(side == 1)
    def _():
        pltpu.make_async_copy(vision_ref, x_nat, local_sem.at[0]).start()

    text_copy = pltpu.make_async_copy(text_ref, text, local_sem.at[1])
    text_copy.start()

    own = here.slab(0, here.y)

    def part(rows, half, i):
        at = pl.multiple_of(i * 1280 + half * HALF, 128)
        return qkv_ref[0, rows, pl.ds(at, HALF)]

    first, rest = pl.ds(0, 16), pl.ds(16, 4)

    def left_of(half):
        return compact(jnp.concatenate([part(rest, half, i).astype(F32) for i in range(3)], axis=1), 512)

    for i in range(3):
        send_q[:, i * HALF : (i + 1) * HALF] = part(first, 1 - h, i)
    send_sq[...] = left_of(1 - h)
    wo[h, own] = out_w_ref[0, pl.ds(0, 16), :]
    small_o[h, here.y] = compact(out_w_ref[0, pl.ds(16, 4), :], 384)
    raw_gains[h] = jnp.broadcast_to(gain_ref[...], (16, 1280))

    pl.semaphore_wait(barrier, len(greet))
    exchange = [
        copies.start(send_q, wq.at[h, own], here.partner()),
        copies.start(send_sq, small_q.at[h, here.y], here.partner()),
        copies.start(wo.at[h, own], wo.at[h, own], here.partner()),
        copies.start(small_o.at[h, here.y], small_o.at[h, here.y], here.partner()),
        copies.start(raw_gains.at[h], raw_gains.at[h], here.partner()),
    ]

    wp[own] = proj_ref[pl.ds(0, 16), :]
    small_p[here.y] = compact(proj_ref[pl.ds(16, 4), :], 512)
    gp = Gather(0, here, copies, wp, small_p, 1536)
    gp.round(0)
    for i in range(3):
        wq[h, own, :, i * HALF : (i + 1) * HALF] = part(first, h, i)
    small_q[h, here.y] = left_of(h)

    a0 = Gather(1, here, copies, wq.at[0], small_q.at[0], 1408)
    a1 = Gather(2, here, copies, wq.at[1], small_q.at[1], 1408)
    b0 = Gather(3, here, copies, wo.at[0], small_o.at[0], 1024)
    b1 = Gather(4, here, copies, wo.at[1], small_o.at[1], 1024)

    for copy in exchange[:2]:
        copy.wait_recv()
    a0.round(0)
    for copy in exchange[2:]:
        copy.wait_recv()

    def prepare_perm():
        t = lax.broadcasted_iota(jnp.int32, (1, HALF), 1)
        u = t - 512
        source = jnp.where(t < 512, (t // 16) * 20 + t % 16, (u // 4) * 20 + 16 + u % 4)
        perm[...] = (lax.broadcasted_iota(jnp.int32, (HALF, HALF), 0) == source).astype(F32).astype(BF)

    def prepare_rows():
        @pl.when(side == 0)
        def _():
            pltpu.make_async_copy(audio_ref, x_nat, local_sem.at[0]).wait()

        @pl.when(side == 1)
        def _():
            pltpu.make_async_copy(vision_ref, x_nat, local_sem.at[0]).wait()

        for b in range(2):
            sl = slice(b * HALF, (b + 1) * HALF)
            for l in range(2):
                gains[l, :, sl] = dot(raw_gains[l, :, sl], perm[...]).astype(BF)
            xp[b] = dot(x_nat[:, sl], perm[...]).astype(BF)

    def prepare_bias():
        ids = jnp.where(side == 0, ids_a_ref[...], ids_v_ref[...])
        hot = (lax.broadcasted_iota(jnp.int32, (16, ROWS), 0) == ids).astype(F32).astype(BF)
        same = lax.dot_general(hot, hot, (((0,), (0,)), ((), ())), preferred_element_type=F32)
        bias[...] = (same - 1.0) * 1e30

    def prepare_place():
        place[...] = (lax.broadcasted_iota(jnp.int32, (768, 512), 0) == order_ref[:, :512]).astype(F32).astype(BF)

    def prepare_text():
        text_copy.wait()

        def body(i, carry):
            at = pl.ds(pl.multiple_of(i * 64, 64), 64)
            taken = jnp.sum(place[at, :].astype(F32), axis=-1, keepdims=True)
            text[at, :] = jnp.where(taken > 0.5, 0.0, text[at, :].astype(F32)).astype(BF)
            return carry

        lax.fori_loop(0, 12, body, 0)

    def norm(l, c):
        def body(i, carry):
            at = pl.ds(pl.multiple_of(c * CHUNK + i * 32, 32), 32)
            a = xp[0, at, :].astype(F32)
            b = xp[1, at, :].astype(F32)
            mean = (jnp.sum(a, axis=-1, keepdims=True) + jnp.sum(b, axis=-1, keepdims=True)) * (1.0 / 1280)
            a = a - mean
            b = b - mean
            var = (jnp.sum(a * a, axis=-1, keepdims=True) + jnp.sum(b * b, axis=-1, keepdims=True)) * (1.0 / 1280)
            scale = lax.rsqrt(var + 1e-05)
            gain = gains[l, pl.ds(0, 16), :].astype(F32)[0:1]
            normed[at, pl.ds(0, HALF)] = (a * scale * gain[:, :HALF]).astype(BF)
            normed[at, pl.ds(HALF, HALF)] = (b * scale * gain[:, HALF:]).astype(BF)
            return carry

        lax.fori_loop(0, CHUNK // 32, body, 0)

    def project(l):
        for i in range(3):
            sl = slice(i * HALF, (i + 1) * HALF)
            packed[:, sl] = dot(normed[...], flat(wq[l, :, :, sl])).astype(BF)

    def head(q, k, v, mask, keep, scale):
        s = lax.dot_general(q, jnp.where(keep, k, 0), (((1,), (1,)), ((), ())), preferred_element_type=F32)
        s = s * scale + mask
        e = jnp.exp(s - jnp.max(s, axis=-1, keepdims=True))
        weights = (e / jnp.sum(e, axis=-1, keepdims=True)).astype(BF)
        return dot(weights, jnp.where(keep, v, 0))

    def attend(l, c):
        at = pl.ds(c * CHUNK, CHUNK)

        @pl.when(side == 0)
        def _():
            def body(j, carry):
                q, k, v = [
                    packed[at if i == 0 else pl.ds(0, ROWS), pl.ds(pl.multiple_of(i * HALF + j * 128, 128), 128)]
                    for i in range(3)
                ]
                low = lax.broadcasted_iota(jnp.int32, (ROWS, 128), 1) < 64
                mask = bias[at, :]
                total = head(q, k, v, mask, low, 0.125) + head(q, k, v, mask, jnp.logical_not(low), 0.125)
                mixed[l, h, at, pl.ds(pl.multiple_of(j * 128, 128), 128)] = total.astype(BF)
                return carry

            lax.fori_loop(0, 5, body, 0)

        @pl.when(side == 1)
        def _():
            macc[...] = jnp.zeros((CHUNK, HALF), F32)
            for i in range(8):
                lo, hi = (80 * i) // 128 * 128, (80 * i + 80 + 127) // 128 * 128
                q, k, v = [packed[at if j == 0 else pl.ds(0, ROWS), j * HALF + lo : j * HALF + hi] for j in range(3)]
                lane = lax.broadcasted_iota(jnp.int32, (ROWS, hi - lo), 1) + lo
                keep = (lane >= 80 * i) & (lane < 80 * i + 80)
                macc[:, lo:hi] = macc[:, lo:hi] + head(q, k, v, bias[at, :], keep, 80 ** (-0.5))
            mixed[l, h, at, :] = macc[...].astype(BF)

        piece = mixed.at[l, h, at, :]
        return copies.start(piece, piece, here.partner())

    def out_layer(l, c, copy, to):
        copy.wait_recv()
        at = pl.ds(c * CHUNK, CHUNK)
        update = None
        for b in range(2):
            rows = dot(mixed[l, b, at, :], perm[...]).astype(BF)
            term = dot(rows, flat(wo[l, pl.ds(40 * b, 40), :, :]))
            update = term if update is None else update + term
        x_new = (x_nat[at, :].astype(F32) + update).astype(BF)
        x_nat[at, :] = x_new
        for b in range(2):
            to[b, at, :] = dot(x_nat[at, pl.ds(b * HALF, HALF)], perm[...]).astype(BF)

    def columns(j):
        return pl.ds(pl.multiple_of(j * 512, 512), 512)

    def own_rows(j, carry):
        cols = columns(j)
        rows = dot(enc[side, 0], flat(wp[pl.ds(0, 40), :, cols])) + dot(enc[side, 1], flat(wp[pl.ds(40, 40), :, cols]))
        spread = dot(place[:, pl.ds(pl.multiple_of(side * ROWS, ROWS), ROWS)], rows.astype(BF))
        text[:, cols] = (text[:, cols].astype(F32) + spread).astype(BF)
        return carry

    def other_rows(j, carry):
        cols = columns(j)
        o = 1 - side
        rows = dot(enc[o, 0], flat(wp[pl.ds(0, 40), :, cols])) + dot(enc[o, 1], flat(wp[pl.ds(40, 40), :, cols]))
        spread = dot(place[:, pl.ds(pl.multiple_of(o * ROWS, ROWS), ROWS)], rows.astype(BF))
        out_buf[:, cols] = (text[:, cols].astype(F32) + spread).astype(BF)
        pltpu.make_async_copy(out_buf.at[:, cols], result_ref.at[:, cols], local_sem.at[2 + j]).start()
        return carry

    b0.round(0)
    prepare_perm()
    a0.round(1)
    b0.round(1)
    gp.round(1)
    prepare_rows()
    a0.round(2)
    b0.round(2)
    a1.round(0)
    prepare_bias()
    a0.round(3)
    b0.round(3)
    a1.round(1)
    gp.round(2)
    prepare_place()
    a0.round(4)
    b0.round(4)
    a1.round(2)
    norm(0, 0)
    norm(0, 1)
    a0.round(5)
    b0.round(5)
    a1.round(3)
    gp.round(3)
    a0.round(6)
    a1.round(4)
    a0.round(7)
    project(0)
    b0.round(6)
    b1.round(0)
    m0 = attend(0, 0)
    m1 = attend(0, 1)
    b0.round(7)
    a1.round(5)
    b1.round(1)
    out_layer(0, 0, m0, xp)
    norm(1, 0)
    a1.round(6)
    b1.round(2)
    gp.round(4)
    out_layer(0, 1, m1, xp)
    norm(1, 1)
    a1.round(7)
    project(1)
    b1.round(3)
    m0 = attend(1, 0)
    m1 = attend(1, 1)
    b1.round(4)
    gp.round(5)
    b1.round(5)
    gp.round(6)
    prepare_text()
    b1.round(6)
    b1.round(7)

    def send_across(c):
        piece = enc.at[side, h, pl.ds(c * CHUNK, CHUNK), :]
        return copies.start(piece, piece, here.across())

    def pass_on(c, copy):
        copy.wait_recv()
        piece = enc.at[1 - side, 1 - h, pl.ds(c * CHUNK, CHUNK), :]
        return copies.start(piece, piece, here.partner())

    mine = enc.at[side]
    out_layer(1, 0, m0, mine)
    e0 = send_across(0)
    out_layer(1, 1, m1, mine)
    e1 = send_across(1)
    gp.round(7)
    f0 = pass_on(0, e0)
    lax.fori_loop(0, 2, own_rows, 0)
    f1 = pass_on(1, e1)
    lax.fori_loop(2, 4, own_rows, 0)
    f0.wait_recv()
    f1.wait_recv()
    lax.fori_loop(0, 4, other_rows, 0)
    copies.finish()
    for gather in (a0, b0, a1, b1, gp):
        gather.finish()
    assert copies.at[0] <= N_SEND and copies.at[1] <= N_RECV
    for j in range(4):
        cols = pl.ds(j * 512, 512)
        pltpu.make_async_copy(out_buf.at[:, cols], result_ref.at[:, cols], local_sem.at[2 + j]).wait()


def per_device(audio, vision, ids_a, ids_v, order, text, gain, qkv, out_w, proj):
    vm = pl.BlockSpec(memory_space=pltpu.VMEM)
    anywhere = pl.BlockSpec(memory_space=pl.ANY)
    return pl.pallas_call(
        kernel,
        out_shape=jax.ShapeDtypeStruct((768, 2048), BF),
        in_specs=[anywhere, anywhere, vm, vm, vm, anywhere, vm, vm, vm, vm],
        out_specs=anywhere,
        scratch_shapes=[
            pltpu.VMEM((2, 80, 16, 1920), BF),
            pltpu.VMEM((2, 80, 16, 1280), BF),
            pltpu.VMEM((80, 16, 2048), BF),
            pltpu.VMEM((2, 4, 16, 512), BF),
            pltpu.VMEM((2, 4, 16, 384), BF),
            pltpu.VMEM((4, 16, 512), BF),
            pltpu.VMEM((16, 1920), BF),
            pltpu.VMEM((16, 512), BF),
            pltpu.VMEM((2, 16, 1280), BF),
            pltpu.VMEM((2, 16, 1280), BF),
            pltpu.VMEM((ROWS, 1280), BF),
            pltpu.VMEM((2, ROWS, HALF), BF),
            pltpu.VMEM((ROWS, ROWS), F32),
            pltpu.VMEM((HALF, HALF), BF),
            pltpu.VMEM((ROWS, 1280), BF),
            pltpu.VMEM((ROWS, 3 * HALF), BF),
            pltpu.VMEM((CHUNK, HALF), F32),
            pltpu.VMEM((2, 2, ROWS, HALF), BF),
            pltpu.VMEM((2, 2, ROWS, HALF), BF),
            pltpu.VMEM((768, 512), BF),
            pltpu.VMEM((768, 2048), BF),
            pltpu.VMEM((768, 2048), BF),
            pltpu.SemaphoreType.DMA((N_SEND,)),
            pltpu.SemaphoreType.DMA((N_RECV,)),
            pltpu.SemaphoreType.DMA((8,)),
        ],
        name="encode",
        compiler_params=pltpu.CompilerParams(collective_id=0, has_side_effects=True, vmem_limit_bytes=56 * 2**20),
        cost_estimate=pl.CostEstimate(flops=12_000_000_000, bytes_accessed=30_000_000, transcendentals=2_000_000),
    )(audio, vision, ids_a, ids_v, order, text, gain, qkv, out_w, proj)


def solution(mesh):
    placed = (
        P(("dp", "fsdp"), None),
        P(("dp", "fsdp"), None),
        P(("dp", "fsdp"), None),
        P(("dp", "fsdp"), None),
        P(("dp", "fsdp"), None),
        P(("dp", "fsdp"), "phase"),
        P("phase", None),
        P("phase", ("dp", "fsdp"), None),
        P("phase", ("dp", "fsdp"), None),
        P(("dp", "fsdp"), "phase"),
    )
    return jax.shard_map(
        per_device,
        mesh=mesh,
        in_specs=placed,
        out_specs=P(("dp", "fsdp"), "phase"),
        check_vma=False,
    )
```

```python
import jax
import jax.numpy as jnp
from jax import lax
from jax.experimental import pallas as pl
from jax.experimental.pallas import tpu as pltpu
from jax.sharding import PartitionSpec as P

MESH = pl.DeviceIdType.MESH
BF = jnp.bfloat16
F32 = jnp.float32
ROWS = 256
HALF = 640
N_SEND = 52
N_RECV = 182
CHUNK = 128


class Copies:
    def __init__(self, send, recv):
        self.send, self.recv = send, recv
        self.at, self.groups, self.sent = [0, 0], {}, []

    def sem(self, kind, name):
        if (kind, name) not in self.groups:
            self.groups[kind, name] = self.at[kind]
            self.at[kind] += 1
        return (self.send, self.recv)[kind].at[self.groups[kind, name]]

    def start(self, src, dst, to, send=None, recv=None):
        alone = send is None
        if alone:
            send = recv = ("alone", len(self.sent))
        copy = pltpu.make_async_remote_copy(
            src_ref=src,
            dst_ref=dst,
            send_sem=self.sem(0, send),
            recv_sem=self.sem(1, recv),
            device_id=to,
            device_id_type=MESH,
        )
        copy.start()
        if alone:
            self.sent.append(copy)
        return copy

    def wait(self, kind, name, size, to):
        copy = pltpu.make_async_remote_copy(
            src_ref=size,
            dst_ref=size,
            send_sem=self.sem(0, name) if kind == 0 else self.send.at[0],
            recv_sem=self.sem(1, name) if kind == 1 else self.recv.at[0],
            device_id=to,
            device_id_type=MESH,
        )
        if kind == 0:
            copy.wait_send()
        else:
            copy.wait_recv()

    def finish(self):
        for copy in self.sent:
            copy.wait_send()


class Place:
    def __init__(self):
        self.p = lax.axis_index("phase")
        self.d = lax.axis_index("dp")
        self.y = lax.axis_index("fsdp")
        self.z = self.d // 2
        self.c = self.d % 2

    def z_at(self, k):
        return (self.z + (k + 8)) % 8

    def y_at(self, k):
        return (self.y + (k + 4)) % 4

    def along_z(self, k):
        return (self.p, self.z_at(k) * 2 + self.c, self.y)

    def along_y(self, k):
        return (self.p, self.d, self.y_at(k))

    def along_x(self, k):
        return ((self.p + (k + 4)) % 4, self.d, self.y)

    def twin(self):
        return (self.p, self.z * 2 + (1 - self.c), self.y)

    def partner(self):
        return self.along_x(1 - 2 * (self.p % 2))

    def across(self):
        return self.along_x(2 * (self.p % 2) - 1)

    def slab(self, k, y, count=None):
        zz = self.z_at(k)
        at = (zz // 4) * 40 + (zz % 4) * 8 + self.c * 4
        return at + y

    def quad(self, k):
        zz = self.z_at(k)
        return (zz // 4) * 40 + (zz % 4) * 8 + self.c * 4

    def left(self, k):
        zz = self.z_at(k)
        return (zz // 4) * 40 + 32 + (zz % 4) * 2 + self.c


class Gather:
    def __init__(self, tag, here, copies, buf, small, cut):
        self.tag = tag
        self.h, self.cp, self.buf, self.small = here, copies, buf, small
        self.width, self.cut = buf.shape[2], cut
        self.short = small.shape[2]
        tiles = cut // 128
        self.mid = (tiles + 1) // 2 * 128

    def reg_p(self, k, y, part=None):
        lo, hi = {None: (0, self.cut), "a": (0, self.mid), "b": (self.mid, self.cut)}[part]
        return self.buf.at[self.h.slab(k, y), :, pl.ds(lo, hi - lo)]

    def reg_q(self, y, part=None):
        mid = self.cut + (self.width - self.cut + 128) // 256 * 128
        lo, hi = {None: (self.cut, self.width), "a": (self.cut, mid), "b": (mid, self.width)}[part]
        return self.buf.at[self.h.slab(0, y), :, pl.ds(lo, hi - lo)]

    def reg_s(self, y, part=None):
        w = self.short
        mid = w // 256 * 128
        lo, hi = {None: (0, w), "a": (0, mid), "b": (mid, w)}[part]
        return self.small.at[y, :, pl.ds(lo, hi - lo)]

    def reg_quad(self, k, part=None):
        lo, n = {None: (0, 4), "a": (0, 2), "b": (2, 2)}[part]
        return self.buf.at[pl.ds(self.h.quad(k) + lo, n), :, pl.ds(self.cut, self.width - self.cut)]

    def reg_left(self, k, part=None):
        half = self.width // 256 * 128
        lo, n = {None: (0, self.width), "a": (0, half), "b": (half, self.width - half)}[part]
        return self.buf.at[self.h.left(k), :, pl.ds(lo, n)]

    def go(self, kind, group, region, to):
        self.cp.start(region, region, to, (self.tag, kind), (self.tag, kind, group))

    def size(self, kind, n):
        if kind[0] == "p":
            return self.buf.at[pl.ds(0, n), :, pl.ds(0, self.cut)]
        if kind == "quad":
            return self.buf.at[pl.ds(0, 4 * n), :, pl.ds(self.cut, self.width - self.cut)]
        if kind == "q":
            return self.buf.at[pl.ds(0, n), :, pl.ds(self.cut, self.width - self.cut)]
        if kind == "s":
            return self.small.at[pl.ds(0, n)]
        return self.buf.at[pl.ds(0, n)]

    def got(self, kind, group, n):
        self.cp.wait(1, (self.tag, kind, group), self.size(kind, n), self.h.twin())

    def finish(self):
        for kind, n in (("pz", 7), ("py", 24), ("quad", 7), ("left", 7), ("s", 3), ("q", 3), ("t", 40)):
            self.cp.wait(0, (self.tag, kind), self.size(kind, n), self.h.twin())

    def p_send_y(self, k):
        h = self.h
        self.go("py", k, self.reg_p(k, h.y), h.along_y(1))
        self.go("py", k, self.reg_p(k, h.y), h.along_y(-1))

    def p_forward_y(self, k):
        h = self.h
        self.got("py", k, 2)
        self.go("py", ("far", k), self.reg_p(k, h.y_at(-1), "a"), h.along_y(1))
        self.go("py", ("far", k), self.reg_p(k, h.y_at(1), "b"), h.along_y(-1))

    def p_end_y(self, k):
        self.got("py", ("far", k), 1)

    def p_send_z(self, k):
        h = self.h
        a, b = (None, None) if k < 3 else ("a", "b")
        self.go("pz", k, self.reg_p(-k, h.y, a), h.along_z(1))
        self.go("pz", k, self.reg_p(k, h.y, b), h.along_z(-1))

    def p_got_z(self, k):
        self.got("pz", k, 2 if k < 3 else 1)

    def q_send_y(self):
        h = self.h
        for tag, reg in (("s", self.reg_s), ("q", self.reg_q)):
            self.go(tag, 0, reg(h.y), h.along_y(1))
            self.go(tag, 0, reg(h.y), h.along_y(-1))

    def q_forward_y(self):
        h = self.h
        for tag, reg in (("s", self.reg_s), ("q", self.reg_q)):
            self.got(tag, 0, 2)
            self.go(tag, 1, reg(h.y_at(-1), "a"), h.along_y(1))
            self.go(tag, 1, reg(h.y_at(1), "b"), h.along_y(-1))

    def q_end_y(self):
        self.got("q", 1, 1)
        self.q_send_z(0, "quad")
        self.got("s", 1, 1)
        self.gather_left()
        self.q_send_z(0, "left")

    def gather_left(self):
        parts = self.small[...].astype(F32)
        own = self.h.left(0)
        for j in range(4):
            lo, hi = j * self.short, min((j + 1) * self.short, self.width)
            rows = jnp.concatenate([parts[i, 4 * j : 4 * j + 4, : hi - lo] for i in range(4)], axis=0)
            self.buf[own, :, lo:hi] = rows.astype(BF)

    def q_send_z(self, k, what):
        h = self.h
        reg = self.reg_quad if what == "quad" else self.reg_left
        a, b = (None, None) if k < 3 else ("a", "b")
        self.go(what, k, reg(-k, a), h.along_z(1))
        self.go(what, k, reg(k, b), h.along_z(-1))

    def q_forward_z(self, k):
        for what in ("quad", "left"):
            self.got(what, k, 2 if k < 3 else 1)
            if k < 3:
                self.q_send_z(k + 1, what)

    def to_twin(self, k):
        h = self.h
        self.go("t", 0, self.buf.at[pl.ds(h.quad(k), 4)], h.twin())
        self.go("t", 0, self.buf.at[h.left(k)], h.twin())

    def round(self, r):
        if r == 0:
            self.q_send_y()
            self.p_send_z(0)
            self.p_send_y(0)
        if r == 1:
            self.p_got_z(0)
            self.p_send_z(1)
            self.q_forward_y()
            self.p_send_y(-1)
            self.p_send_y(1)
            self.p_forward_y(0)
        if r == 2:
            self.q_end_y()
            self.p_got_z(1)
            self.p_send_z(2)
            self.p_send_y(-2)
            self.p_send_y(2)
            self.p_forward_y(-1)
            self.p_forward_y(1)
        if r == 3:
            self.p_got_z(2)
            self.p_send_z(3)
            self.q_forward_z(0)
            self.p_send_y(-3)
            self.p_send_y(3)
            self.p_forward_y(-2)
            self.p_forward_y(2)
            self.p_end_y(0)
            self.to_twin(0)
        if r == 4:
            self.p_got_z(3)
            self.p_send_y(4)
            self.q_forward_z(1)
            self.p_forward_y(-3)
            self.p_forward_y(3)
            self.p_end_y(-1)
            self.p_end_y(1)
            self.to_twin(-1)
            self.to_twin(1)
        if r == 5:
            self.q_forward_z(2)
            self.p_forward_y(4)
            self.p_end_y(-2)
            self.p_end_y(2)
            self.to_twin(-2)
            self.to_twin(2)
        if r == 6:
            self.q_forward_z(3)
            self.p_end_y(-3)
            self.p_end_y(3)
            self.to_twin(-3)
            self.to_twin(3)
            self.p_end_y(4)
            self.to_twin(4)
        if r == 7:
            self.got("t", 0, 40)


def flat(slabs):
    return slabs.reshape(slabs.shape[0] * slabs.shape[1], slabs.shape[2])


def dot(a, b):
    return jnp.dot(a, b, preferred_element_type=F32)


def compact(rows, short):
    rows = rows.astype(F32)
    fill = 4 * short - rows.shape[1]
    if fill:
        rows = jnp.concatenate([rows, jnp.zeros((4, fill), F32)], axis=1)
    return jnp.concatenate([rows[:, j * short : (j + 1) * short] for j in range(4)], axis=0).astype(BF)


def kernel(
    audio_ref, vision_ref, ids_a_ref, ids_v_ref, order_ref, text_ref, gain_ref, qkv_ref, out_w_ref, proj_ref,
    result_ref,
    wq, wo, wp, small_q, small_o, small_p, send_q, send_sq, raw_gains, gains,
    x_nat, xp, bias, perm, normed, packed, macc, mixed, enc, place, text, out_buf,
    send_sem, recv_sem, local_sem,
):
    here = Place()
    h = here.p % 2
    side = here.p // 2
    copies = Copies(send_sem, recv_sem)

    barrier = pltpu.get_barrier_semaphore()
    greet = [here.along_z(1), here.along_z(-1), here.along_y(1), here.along_y(-1), here.along_x(1), here.along_x(-1), here.twin()]
    for to in greet:
        pl.semaphore_signal(barrier, inc=1, device_id=to, device_id_type=MESH)

    @pl.when(side == 0)
    def _():
        pltpu.make_async_copy(audio_ref, x_nat, local_sem.at[0]).start()

    @pl.when(side == 1)
    def _():
        pltpu.make_async_copy(vision_ref, x_nat, local_sem.at[0]).start()

    text_copy = pltpu.make_async_copy(text_ref, text, local_sem.at[1])
    text_copy.start()

    own = here.slab(0, here.y)

    def part(rows, half, i):
        at = pl.multiple_of(i * 1280 + half * HALF, 128)
        return qkv_ref[0, rows, pl.ds(at, HALF)]

    first, rest = pl.ds(0, 16), pl.ds(16, 4)

    def left_of(half):
        return compact(jnp.concatenate([part(rest, half, i).astype(F32) for i in range(3)], axis=1), 512)

    for i in range(3):
        send_q[:, i * HALF : (i + 1) * HALF] = part(first, 1 - h, i)
    send_sq[...] = left_of(1 - h)
    wo[h, own] = out_w_ref[0, pl.ds(0, 16), :]
    small_o[h, here.y] = compact(out_w_ref[0, pl.ds(16, 4), :], 384)
    raw_gains[h] = jnp.broadcast_to(gain_ref[...], (16, 1280))

    pl.semaphore_wait(barrier, len(greet))
    exchange = [
        copies.start(send_q, wq.at[h, own], here.partner()),
        copies.start(send_sq, small_q.at[h, here.y], here.partner()),
        copies.start(wo.at[h, own], wo.at[h, own], here.partner()),
        copies.start(small_o.at[h, here.y], small_o.at[h, here.y], here.partner()),
        copies.start(raw_gains.at[h], raw_gains.at[h], here.partner()),
    ]

    wp[own] = proj_ref[pl.ds(0, 16), :]
    small_p[here.y] = compact(proj_ref[pl.ds(16, 4), :], 512)
    gp = Gather(0, here, copies, wp, small_p, 1536)
    gp.round(0)
    for i in range(3):
        wq[h, own, :, i * HALF : (i + 1) * HALF] = part(first, h, i)
    small_q[h, here.y] = left_of(h)

    a0 = Gather(1, here, copies, wq.at[0], small_q.at[0], 1408)
    a1 = Gather(2, here, copies, wq.at[1], small_q.at[1], 1408)
    b0 = Gather(3, here, copies, wo.at[0], small_o.at[0], 1024)
    b1 = Gather(4, here, copies, wo.at[1], small_o.at[1], 1024)

    for copy in exchange[:2]:
        copy.wait_recv()
    a0.round(0)
    for copy in exchange[2:]:
        copy.wait_recv()

    def prepare_perm():
        t = lax.broadcasted_iota(jnp.int32, (1, HALF), 1)
        u = t - 512
        source = jnp.where(t < 512, (t // 16) * 20 + t % 16, (u // 4) * 20 + 16 + u % 4)
        perm[...] = (lax.broadcasted_iota(jnp.int32, (HALF, HALF), 0) == source).astype(F32).astype(BF)

    def prepare_rows():
        @pl.when(side == 0)
        def _():
            pltpu.make_async_copy(audio_ref, x_nat, local_sem.at[0]).wait()

        @pl.when(side == 1)
        def _():
            pltpu.make_async_copy(vision_ref, x_nat, local_sem.at[0]).wait()

        for b in range(2):
            sl = slice(b * HALF, (b + 1) * HALF)
            for l in range(2):
                gains[l, :, sl] = dot(raw_gains[l, :, sl], perm[...]).astype(BF)
            xp[b] = dot(x_nat[:, sl], perm[...]).astype(BF)

    def prepare_bias():
        ids = jnp.where(side == 0, ids_a_ref[...], ids_v_ref[...])
        hot = (lax.broadcasted_iota(jnp.int32, (16, ROWS), 0) == ids).astype(F32).astype(BF)
        same = lax.dot_general(hot, hot, (((0,), (0,)), ((), ())), preferred_element_type=F32)
        bias[...] = (same - 1.0) * 1e30

    def prepare_place():
        place[...] = (lax.broadcasted_iota(jnp.int32, (768, 512), 0) == order_ref[:, :512]).astype(F32).astype(BF)

    def prepare_text():
        text_copy.wait()

        def body(i, carry):
            at = pl.ds(pl.multiple_of(i * 64, 64), 64)
            taken = jnp.sum(place[at, :].astype(F32), axis=-1, keepdims=True)
            text[at, :] = jnp.where(taken > 0.5, 0.0, text[at, :].astype(F32)).astype(BF)
            return carry

        lax.fori_loop(0, 12, body, 0)

    def norm(l, c):
        def body(i, carry):
            at = pl.ds(pl.multiple_of(c * CHUNK + i * 32, 32), 32)
            a = xp[0, at, :].astype(F32)
            b = xp[1, at, :].astype(F32)
            mean = (jnp.sum(a, axis=-1, keepdims=True) + jnp.sum(b, axis=-1, keepdims=True)) * (1.0 / 1280)
            a = a - mean
            b = b - mean
            var = (jnp.sum(a * a, axis=-1, keepdims=True) + jnp.sum(b * b, axis=-1, keepdims=True)) * (1.0 / 1280)
            scale = lax.rsqrt(var + 1e-05)
            gain = gains[l, pl.ds(0, 16), :].astype(F32)[0:1]
            normed[at, pl.ds(0, HALF)] = (a * scale * gain[:, :HALF]).astype(BF)
            normed[at, pl.ds(HALF, HALF)] = (b * scale * gain[:, HALF:]).astype(BF)
            return carry

        lax.fori_loop(0, CHUNK // 32, body, 0)

    def project(l):
        for i in range(3):
            sl = slice(i * HALF, (i + 1) * HALF)
            packed[:, sl] = dot(normed[...], flat(wq[l, :, :, sl])).astype(BF)

    def head(q, k, v, mask, keep, scale):
        s = lax.dot_general(q, jnp.where(keep, k, 0), (((1,), (1,)), ((), ())), preferred_element_type=F32)
        s = s * scale + mask
        e = jnp.exp(s - jnp.max(s, axis=-1, keepdims=True))
        weights = (e / jnp.sum(e, axis=-1, keepdims=True)).astype(BF)
        return dot(weights, jnp.where(keep, v, 0))

    def attend(l, c):
        at = pl.ds(c * CHUNK, CHUNK)

        @pl.when(side == 0)
        def _():
            def body(j, carry):
                q, k, v = [
                    packed[at if i == 0 else pl.ds(0, ROWS), pl.ds(pl.multiple_of(i * HALF + j * 128, 128), 128)]
                    for i in range(3)
                ]
                low = lax.broadcasted_iota(jnp.int32, (ROWS, 128), 1) < 64
                mask = bias[at, :]
                total = head(q, k, v, mask, low, 0.125) + head(q, k, v, mask, jnp.logical_not(low), 0.125)
                mixed[l, h, at, pl.ds(pl.multiple_of(j * 128, 128), 128)] = total.astype(BF)
                return carry

            lax.fori_loop(0, 5, body, 0)

        @pl.when(side == 1)
        def _():
            macc[...] = jnp.zeros((CHUNK, HALF), F32)
            for i in range(8):
                lo, hi = (80 * i) // 128 * 128, (80 * i + 80 + 127) // 128 * 128
                q, k, v = [packed[at if j == 0 else pl.ds(0, ROWS), j * HALF + lo : j * HALF + hi] for j in range(3)]
                lane = lax.broadcasted_iota(jnp.int32, (ROWS, hi - lo), 1) + lo
                keep = (lane >= 80 * i) & (lane < 80 * i + 80)
                macc[:, lo:hi] = macc[:, lo:hi] + head(q, k, v, bias[at, :], keep, 80 ** (-0.5))
            mixed[l, h, at, :] = macc[...].astype(BF)

        piece = mixed.at[l, h, at, :]
        return copies.start(piece, piece, here.partner())

    def out_layer(l, c, copy, to):
        copy.wait_recv()
        at = pl.ds(c * CHUNK, CHUNK)
        update = None
        for b in range(2):
            rows = dot(mixed[l, b, at, :], perm[...]).astype(BF)
            term = dot(rows, flat(wo[l, pl.ds(40 * b, 40), :, :]))
            update = term if update is None else update + term
        x_new = (x_nat[at, :].astype(F32) + update).astype(BF)
        x_nat[at, :] = x_new
        for b in range(2):
            to[b, at, :] = dot(x_nat[at, pl.ds(b * HALF, HALF)], perm[...]).astype(BF)

    def columns(j):
        return pl.ds(pl.multiple_of(j * 512, 512), 512)

    def own_rows(j, carry):
        cols = columns(j)
        rows = dot(enc[side, 0], flat(wp[pl.ds(0, 40), :, cols])) + dot(enc[side, 1], flat(wp[pl.ds(40, 40), :, cols]))
        spread = dot(place[:, pl.ds(pl.multiple_of(side * ROWS, ROWS), ROWS)], rows.astype(BF))
        text[:, cols] = (text[:, cols].astype(F32) + spread).astype(BF)
        return carry

    def other_rows(j, carry):
        cols = columns(j)
        o = 1 - side
        rows = dot(enc[o, 0], flat(wp[pl.ds(0, 40), :, cols])) + dot(enc[o, 1], flat(wp[pl.ds(40, 40), :, cols]))
        spread = dot(place[:, pl.ds(pl.multiple_of(o * ROWS, ROWS), ROWS)], rows.astype(BF))
        out_buf[:, cols] = (text[:, cols].astype(F32) + spread).astype(BF)
        pltpu.make_async_copy(out_buf.at[:, cols], result_ref.at[:, cols], local_sem.at[2 + j]).start()
        return carry

    b0.round(0)
    prepare_perm()
    a0.round(1)
    b0.round(1)
    gp.round(1)
    prepare_rows()
    a0.round(2)
    b0.round(2)
    a1.round(0)
    prepare_bias()
    a0.round(3)
    b0.round(3)
    a1.round(1)
    gp.round(2)
    prepare_place()
    a0.round(4)
    b0.round(4)
    a1.round(2)
    norm(0, 0)
    norm(0, 1)
    a0.round(5)
    b0.round(5)
    a1.round(3)
    gp.round(3)
    a0.round(6)
    a1.round(4)
    a0.round(7)
    project(0)
    b0.round(6)
    b1.round(0)
    m0 = attend(0, 0)
    m1 = attend(0, 1)
    b0.round(7)
    a1.round(5)
    b1.round(1)
    out_layer(0, 0, m0, xp)
    norm(1, 0)
    a1.round(6)
    b1.round(2)
    gp.round(4)
    out_layer(0, 1, m1, xp)
    norm(1, 1)
    a1.round(7)
    project(1)
    b1.round(3)
    m0 = attend(1, 0)
    m1 = attend(1, 1)
    b1.round(4)
    gp.round(5)
    b1.round(5)
    gp.round(6)
    prepare_text()
    b1.round(6)
    b1.round(7)

    def send_across(c):
        piece = enc.at[side, h, pl.ds(c * 64, 64), :]
        return copies.start(piece, piece, here.across())

    def pass_on(c, copy):
        copy.wait_recv()
        piece = enc.at[1 - side, 1 - h, pl.ds(c * 64, 64), :]
        return copies.start(piece, piece, here.partner())

    mine = enc.at[side]
    out_layer(1, 0, m0, mine)
    e0 = [send_across(0), send_across(1)]
    out_layer(1, 1, m1, mine)
    e1 = [send_across(2), send_across(3)]
    gp.round(7)
    f0 = [pass_on(0, e0[0]), pass_on(1, e0[1])]
    lax.fori_loop(0, 1, own_rows, 0)
    f1 = [pass_on(2, e1[0])]
    lax.fori_loop(1, 2, own_rows, 0)
    f1.append(pass_on(3, e1[1]))
    lax.fori_loop(2, 4, own_rows, 0)
    for copy in f0 + f1:
        copy.wait_recv()
    lax.fori_loop(0, 4, other_rows, 0)
    copies.finish()
    for gather in (a0, b0, a1, b1, gp):
        gather.finish()
    assert copies.at[0] <= N_SEND and copies.at[1] <= N_RECV
    for j in range(4):
        cols = pl.ds(j * 512, 512)
        pltpu.make_async_copy(out_buf.at[:, cols], result_ref.at[:, cols], local_sem.at[2 + j]).wait()


def per_device(audio, vision, ids_a, ids_v, order, text, gain, qkv, out_w, proj):
    vm = pl.BlockSpec(memory_space=pltpu.VMEM)
    anywhere = pl.BlockSpec(memory_space=pl.ANY)
    return pl.pallas_call(
        kernel,
        out_shape=jax.ShapeDtypeStruct((768, 2048), BF),
        in_specs=[anywhere, anywhere, vm, vm, vm, anywhere, vm, vm, vm, vm],
        out_specs=anywhere,
        scratch_shapes=[
            pltpu.VMEM((2, 80, 16, 1920), BF),
            pltpu.VMEM((2, 80, 16, 1280), BF),
            pltpu.VMEM((80, 16, 2048), BF),
            pltpu.VMEM((2, 4, 16, 512), BF),
            pltpu.VMEM((2, 4, 16, 384), BF),
            pltpu.VMEM((4, 16, 512), BF),
            pltpu.VMEM((16, 1920), BF),
            pltpu.VMEM((16, 512), BF),
            pltpu.VMEM((2, 16, 1280), BF),
            pltpu.VMEM((2, 16, 1280), BF),
            pltpu.VMEM((ROWS, 1280), BF),
            pltpu.VMEM((2, ROWS, HALF), BF),
            pltpu.VMEM((ROWS, ROWS), F32),
            pltpu.VMEM((HALF, HALF), BF),
            pltpu.VMEM((ROWS, 1280), BF),
            pltpu.VMEM((ROWS, 3 * HALF), BF),
            pltpu.VMEM((CHUNK, HALF), F32),
            pltpu.VMEM((2, 2, ROWS, HALF), BF),
            pltpu.VMEM((2, 2, ROWS, HALF), BF),
            pltpu.VMEM((768, 512), BF),
            pltpu.VMEM((768, 2048), BF),
            pltpu.VMEM((768, 2048), BF),
            pltpu.SemaphoreType.DMA((N_SEND,)),
            pltpu.SemaphoreType.DMA((N_RECV,)),
            pltpu.SemaphoreType.DMA((8,)),
        ],
        name="encode",
        compiler_params=pltpu.CompilerParams(collective_id=0, has_side_effects=True, vmem_limit_bytes=56 * 2**20),
        cost_estimate=pl.CostEstimate(flops=12_000_000_000, bytes_accessed=30_000_000, transcendentals=2_000_000),
    )(audio, vision, ids_a, ids_v, order, text, gain, qkv, out_w, proj)


def solution(mesh):
    placed = (
        P(("dp", "fsdp"), None),
        P(("dp", "fsdp"), None),
        P(("dp", "fsdp"), None),
        P(("dp", "fsdp"), None),
        P(("dp", "fsdp"), None),
        P(("dp", "fsdp"), "phase"),
        P("phase", None),
        P("phase", ("dp", "fsdp"), None),
        P("phase", ("dp", "fsdp"), None),
        P(("dp", "fsdp"), "phase"),
    )
    return jax.shard_map(
        per_device,
        mesh=mesh,
        in_specs=placed,
        out_specs=P(("dp", "fsdp"), "phase"),
        check_vma=False,
    )
```

```python
import jax
import jax.numpy as jnp
from jax import lax
from jax.experimental import pallas as pl
from jax.experimental.pallas import tpu as pltpu
from jax.sharding import PartitionSpec as P

MESH = pl.DeviceIdType.MESH
BF = jnp.bfloat16
F32 = jnp.float32
ROWS = 256
HALF = 640
N_SEND = 52
N_RECV = 182
CHUNK = 128


class Copies:
    def __init__(self, send, recv):
        self.send, self.recv = send, recv
        self.at, self.groups, self.sent = [0, 0], {}, []

    def sem(self, kind, name):
        if (kind, name) not in self.groups:
            self.groups[kind, name] = self.at[kind]
            self.at[kind] += 1
        return (self.send, self.recv)[kind].at[self.groups[kind, name]]

    def start(self, src, dst, to, send=None, recv=None):
        alone = send is None
        if alone:
            send = recv = ("alone", len(self.sent))
        copy = pltpu.make_async_remote_copy(
            src_ref=src,
            dst_ref=dst,
            send_sem=self.sem(0, send),
            recv_sem=self.sem(1, recv),
            device_id=to,
            device_id_type=MESH,
        )
        copy.start()
        if alone:
            self.sent.append(copy)
        return copy

    def wait(self, kind, name, size, to):
        copy = pltpu.make_async_remote_copy(
            src_ref=size,
            dst_ref=size,
            send_sem=self.sem(0, name) if kind == 0 else self.send.at[0],
            recv_sem=self.sem(1, name) if kind == 1 else self.recv.at[0],
            device_id=to,
            device_id_type=MESH,
        )
        if kind == 0:
            copy.wait_send()
        else:
            copy.wait_recv()

    def finish(self):
        for copy in self.sent:
            copy.wait_send()


class Place:
    def __init__(self):
        self.p = lax.axis_index("phase")
        self.d = lax.axis_index("dp")
        self.y = lax.axis_index("fsdp")
        self.z = self.d // 2
        self.c = self.d % 2

    def z_at(self, k):
        return (self.z + (k + 8)) % 8

    def y_at(self, k):
        return (self.y + (k + 4)) % 4

    def along_z(self, k):
        return (self.p, self.z_at(k) * 2 + self.c, self.y)

    def along_y(self, k):
        return (self.p, self.d, self.y_at(k))

    def along_x(self, k):
        return ((self.p + (k + 4)) % 4, self.d, self.y)

    def twin(self):
        return (self.p, self.z * 2 + (1 - self.c), self.y)

    def partner(self):
        return self.along_x(1 - 2 * (self.p % 2))

    def across(self):
        return self.along_x(2 * (self.p % 2) - 1)

    def slab(self, k, y, count=None):
        zz = self.z_at(k)
        at = (zz // 4) * 40 + (zz % 4) * 8 + self.c * 4
        return at + y

    def quad(self, k):
        zz = self.z_at(k)
        return (zz // 4) * 40 + (zz % 4) * 8 + self.c * 4

    def left(self, k):
        zz = self.z_at(k)
        return (zz // 4) * 40 + 32 + (zz % 4) * 2 + self.c


class Gather:
    def __init__(self, tag, here, copies, buf, small, cut):
        self.tag = tag
        self.h, self.cp, self.buf, self.small = here, copies, buf, small
        self.width, self.cut = buf.shape[2], cut
        self.short = small.shape[2]
        tiles = cut // 128
        self.mid = (tiles + 1) // 2 * 128

    def reg_p(self, k, y, part=None):
        lo, hi = {None: (0, self.cut), "a": (0, self.mid), "b": (self.mid, self.cut)}[part]
        return self.buf.at[self.h.slab(k, y), :, pl.ds(lo, hi - lo)]

    def reg_q(self, y, part=None):
        mid = self.cut + (self.width - self.cut + 128) // 256 * 128
        lo, hi = {None: (self.cut, self.width), "a": (self.cut, mid), "b": (mid, self.width)}[part]
        return self.buf.at[self.h.slab(0, y), :, pl.ds(lo, hi - lo)]

    def reg_s(self, y, part=None):
        w = self.short
        mid = w // 256 * 128
        lo, hi = {None: (0, w), "a": (0, mid), "b": (mid, w)}[part]
        return self.small.at[y, :, pl.ds(lo, hi - lo)]

    def reg_quad(self, k, part=None):
        lo, n = {None: (0, 4), "a": (0, 2), "b": (2, 2)}[part]
        return self.buf.at[pl.ds(self.h.quad(k) + lo, n), :, pl.ds(self.cut, self.width - self.cut)]

    def reg_left(self, k, part=None):
        half = self.width // 256 * 128
        lo, n = {None: (0, self.width), "a": (0, half), "b": (half, self.width - half)}[part]
        return self.buf.at[self.h.left(k), :, pl.ds(lo, n)]

    def go(self, kind, group, region, to):
        self.cp.start(region, region, to, (self.tag, kind), (self.tag, kind, group))

    def size(self, kind, n):
        if kind[0] == "p":
            return self.buf.at[pl.ds(0, n), :, pl.ds(0, self.cut)]
        if kind == "quad":
            return self.buf.at[pl.ds(0, 4 * n), :, pl.ds(self.cut, self.width - self.cut)]
        if kind == "q":
            return self.buf.at[pl.ds(0, n), :, pl.ds(self.cut, self.width - self.cut)]
        if kind == "s":
            return self.small.at[pl.ds(0, n)]
        return self.buf.at[pl.ds(0, n)]

    def got(self, kind, group, n):
        self.cp.wait(1, (self.tag, kind, group), self.size(kind, n), self.h.twin())

    def finish(self):
        for kind, n in (("pz", 7), ("py", 24), ("quad", 7), ("left", 7), ("s", 3), ("q", 3), ("t", 40)):
            self.cp.wait(0, (self.tag, kind), self.size(kind, n), self.h.twin())

    def p_send_y(self, k):
        h = self.h
        self.go("py", k, self.reg_p(k, h.y), h.along_y(1))
        self.go("py", k, self.reg_p(k, h.y), h.along_y(-1))

    def p_forward_y(self, k):
        h = self.h
        self.got("py", k, 2)
        self.go("py", ("far", k), self.reg_p(k, h.y_at(-1), "a"), h.along_y(1))
        self.go("py", ("far", k), self.reg_p(k, h.y_at(1), "b"), h.along_y(-1))

    def p_end_y(self, k):
        self.got("py", ("far", k), 1)

    def p_send_z(self, k):
        h = self.h
        a, b = (None, None) if k < 3 else ("a", "b")
        self.go("pz", k, self.reg_p(-k, h.y, a), h.along_z(1))
        self.go("pz", k, self.reg_p(k, h.y, b), h.along_z(-1))

    def p_got_z(self, k):
        self.got("pz", k, 2 if k < 3 else 1)

    def q_send_y(self):
        h = self.h
        for tag, reg in (("s", self.reg_s), ("q", self.reg_q)):
            self.go(tag, 0, reg(h.y), h.along_y(1))
            self.go(tag, 0, reg(h.y), h.along_y(-1))

    def q_forward_y(self):
        h = self.h
        for tag, reg in (("s", self.reg_s), ("q", self.reg_q)):
            self.got(tag, 0, 2)
            self.go(tag, 1, reg(h.y_at(-1), "a"), h.along_y(1))
            self.go(tag, 1, reg(h.y_at(1), "b"), h.along_y(-1))

    def q_end_y(self):
        self.got("q", 1, 1)
        self.q_send_z(0, "quad")
        self.got("s", 1, 1)
        self.gather_left()
        self.q_send_z(0, "left")

    def gather_left(self):
        parts = self.small[...].astype(F32)
        own = self.h.left(0)
        for j in range(4):
            lo, hi = j * self.short, min((j + 1) * self.short, self.width)
            rows = jnp.concatenate([parts[i, 4 * j : 4 * j + 4, : hi - lo] for i in range(4)], axis=0)
            self.buf[own, :, lo:hi] = rows.astype(BF)

    def q_send_z(self, k, what):
        h = self.h
        reg = self.reg_quad if what == "quad" else self.reg_left
        a, b = (None, None) if k < 3 else ("a", "b")
        self.go(what, k, reg(-k, a), h.along_z(1))
        self.go(what, k, reg(k, b), h.along_z(-1))

    def q_forward_z(self, k):
        for what in ("quad", "left"):
            self.got(what, k, 2 if k < 3 else 1)
            if k < 3:
                self.q_send_z(k + 1, what)

    def to_twin(self, k):
        h = self.h
        self.go("t", 0, self.buf.at[pl.ds(h.quad(k), 4)], h.twin())
        self.go("t", 0, self.buf.at[h.left(k)], h.twin())

    def round(self, r):
        if r == 0:
            self.q_send_y()
            self.p_send_z(0)
            self.p_send_y(0)
        if r == 1:
            self.p_got_z(0)
            self.p_send_z(1)
            self.q_forward_y()
            self.p_send_y(-1)
            self.p_send_y(1)
            self.p_forward_y(0)
        if r == 2:
            self.q_end_y()
            self.p_got_z(1)
            self.p_send_z(2)
            self.p_send_y(-2)
            self.p_send_y(2)
            self.p_forward_y(-1)
            self.p_forward_y(1)
        if r == 3:
            self.p_got_z(2)
            self.p_send_z(3)
            self.q_forward_z(0)
            self.p_send_y(-3)
            self.p_send_y(3)
            self.p_forward_y(-2)
            self.p_forward_y(2)
            self.p_end_y(0)
            self.to_twin(0)
        if r == 4:
            self.p_got_z(3)
            self.p_send_y(4)
            self.q_forward_z(1)
            self.p_forward_y(-3)
            self.p_forward_y(3)
            self.p_end_y(-1)
            self.p_end_y(1)
            self.to_twin(-1)
            self.to_twin(1)
        if r == 5:
            self.q_forward_z(2)
            self.p_forward_y(4)
            self.p_end_y(-2)
            self.p_end_y(2)
            self.to_twin(-2)
            self.to_twin(2)
        if r == 6:
            self.q_forward_z(3)
            self.p_end_y(-3)
            self.p_end_y(3)
            self.to_twin(-3)
            self.to_twin(3)
            self.p_end_y(4)
            self.to_twin(4)
        if r == 7:
            self.got("t", 0, 40)


def flat(slabs):
    return slabs.reshape(slabs.shape[0] * slabs.shape[1], slabs.shape[2])


def dot(a, b):
    return jnp.dot(a, b, preferred_element_type=F32)


def compact(rows, short):
    rows = rows.astype(F32)
    fill = 4 * short - rows.shape[1]
    if fill:
        rows = jnp.concatenate([rows, jnp.zeros((4, fill), F32)], axis=1)
    return jnp.concatenate([rows[:, j * short : (j + 1) * short] for j in range(4)], axis=0).astype(BF)


def kernel(
    audio_ref, vision_ref, ids_a_ref, ids_v_ref, order_ref, text_ref, gain_ref, qkv_ref, out_w_ref, proj_ref,
    result_ref,
    wq, wo, wp, small_q, small_o, small_p, send_q, send_sq, raw_gains, gains,
    x_nat, xp, bias, perm, normed, packed, macc, mixed, enc, place, text, out_buf,
    send_sem, recv_sem, local_sem,
):
    here = Place()
    h = here.p % 2
    side = here.p // 2
    copies = Copies(send_sem, recv_sem)

    barrier = pltpu.get_barrier_semaphore()
    greet = [here.along_z(1), here.along_z(-1), here.along_y(1), here.along_y(-1), here.along_x(1), here.along_x(-1), here.twin()]
    for to in greet:
        pl.semaphore_signal(barrier, inc=1, device_id=to, device_id_type=MESH)

    @pl.when(side == 0)
    def _():
        pltpu.make_async_copy(audio_ref, x_nat, local_sem.at[0]).start()

    @pl.when(side == 1)
    def _():
        pltpu.make_async_copy(vision_ref, x_nat, local_sem.at[0]).start()

    text_copy = pltpu.make_async_copy(text_ref, text, local_sem.at[1])
    text_copy.start()

    own = here.slab(0, here.y)

    def part(rows, half, i):
        at = pl.multiple_of(i * 1280 + half * HALF, 128)
        return qkv_ref[0, rows, pl.ds(at, HALF)]

    first, rest = pl.ds(0, 16), pl.ds(16, 4)

    def left_of(half):
        return compact(jnp.concatenate([part(rest, half, i).astype(F32) for i in range(3)], axis=1), 512)

    for i in range(3):
        send_q[:, i * HALF : (i + 1) * HALF] = part(first, 1 - h, i)
    send_sq[...] = left_of(1 - h)
    wo[h, own] = out_w_ref[0, pl.ds(0, 16), :]
    small_o[h, here.y] = compact(out_w_ref[0, pl.ds(16, 4), :], 384)
    raw_gains[h] = jnp.broadcast_to(gain_ref[...], (16, 1280))

    pl.semaphore_wait(barrier, len(greet))
    exchange = [
        copies.start(send_q, wq.at[h, own], here.partner()),
        copies.start(send_sq, small_q.at[h, here.y], here.partner()),
        copies.start(wo.at[h, own], wo.at[h, own], here.partner()),
        copies.start(small_o.at[h, here.y], small_o.at[h, here.y], here.partner()),
        copies.start(raw_gains.at[h], raw_gains.at[h], here.partner()),
    ]

    wp[own] = proj_ref[pl.ds(0, 16), :]
    small_p[here.y] = compact(proj_ref[pl.ds(16, 4), :], 512)
    gp = Gather(0, here, copies, wp, small_p, 1536)
    gp.round(0)
    for i in range(3):
        wq[h, own, :, i * HALF : (i + 1) * HALF] = part(first, h, i)
    small_q[h, here.y] = left_of(h)

    a0 = Gather(1, here, copies, wq.at[0], small_q.at[0], 1408)
    a1 = Gather(2, here, copies, wq.at[1], small_q.at[1], 1408)
    b0 = Gather(3, here, copies, wo.at[0], small_o.at[0], 1024)
    b1 = Gather(4, here, copies, wo.at[1], small_o.at[1], 1024)

    for copy in exchange[:2]:
        copy.wait_recv()
    a0.round(0)
    for copy in exchange[2:]:
        copy.wait_recv()

    def prepare_perm():
        t = lax.broadcasted_iota(jnp.int32, (1, HALF), 1)
        u = t - 512
        source = jnp.where(t < 512, (t // 16) * 20 + t % 16, (u // 4) * 20 + 16 + u % 4)
        perm[...] = (lax.broadcasted_iota(jnp.int32, (HALF, HALF), 0) == source).astype(F32).astype(BF)

    def prepare_rows():
        @pl.when(side == 0)
        def _():
            pltpu.make_async_copy(audio_ref, x_nat, local_sem.at[0]).wait()

        @pl.when(side == 1)
        def _():
            pltpu.make_async_copy(vision_ref, x_nat, local_sem.at[0]).wait()

        for b in range(2):
            sl = slice(b * HALF, (b + 1) * HALF)
            for l in range(2):
                gains[l, :, sl] = dot(raw_gains[l, :, sl], perm[...]).astype(BF)
            xp[b] = dot(x_nat[:, sl], perm[...]).astype(BF)

    def prepare_bias():
        ids = jnp.where(side == 0, ids_a_ref[...], ids_v_ref[...])
        hot = (lax.broadcasted_iota(jnp.int32, (16, ROWS), 0) == ids).astype(F32).astype(BF)
        same = lax.dot_general(hot, hot, (((0,), (0,)), ((), ())), preferred_element_type=F32)
        bias[...] = (same - 1.0) * 1e30

    def prepare_place():
        place[...] = (lax.broadcasted_iota(jnp.int32, (768, 512), 0) == order_ref[:, :512]).astype(F32).astype(BF)

    def prepare_text():
        text_copy.wait()

        def body(i, carry):
            at = pl.ds(pl.multiple_of(i * 64, 64), 64)
            taken = jnp.sum(place[at, :].astype(F32), axis=-1, keepdims=True)
            text[at, :] = jnp.where(taken > 0.5, 0.0, text[at, :].astype(F32)).astype(BF)
            return carry

        lax.fori_loop(0, 12, body, 0)

    def norm(l, c):
        def body(i, carry):
            at = pl.ds(pl.multiple_of(c * CHUNK + i * 32, 32), 32)
            a = xp[0, at, :].astype(F32)
            b = xp[1, at, :].astype(F32)
            mean = (jnp.sum(a, axis=-1, keepdims=True) + jnp.sum(b, axis=-1, keepdims=True)) * (1.0 / 1280)
            a = a - mean
            b = b - mean
            var = (jnp.sum(a * a, axis=-1, keepdims=True) + jnp.sum(b * b, axis=-1, keepdims=True)) * (1.0 / 1280)
            scale = lax.rsqrt(var + 1e-05)
            gain = gains[l, pl.ds(0, 16), :].astype(F32)[0:1]
            normed[at, pl.ds(0, HALF)] = (a * scale * gain[:, :HALF]).astype(BF)
            normed[at, pl.ds(HALF, HALF)] = (b * scale * gain[:, HALF:]).astype(BF)
            return carry

        lax.fori_loop(0, CHUNK // 32, body, 0)

    def project(l):
        for i in range(3):
            sl = slice(i * HALF, (i + 1) * HALF)
            packed[:, sl] = dot(normed[...], flat(wq[l, :, :, sl])).astype(BF)

    def head(q, k, v, mask, keep, scale):
        s = lax.dot_general(q, jnp.where(keep, k, 0), (((1,), (1,)), ((), ())), preferred_element_type=F32)
        s = s * scale + mask
        e = jnp.exp(s - jnp.max(s, axis=-1, keepdims=True))
        weights = (e * (1.0 / jnp.sum(e, axis=-1, keepdims=True))).astype(BF)
        return dot(weights, jnp.where(keep, v, 0))

    def attend(l, c):
        at = pl.ds(c * CHUNK, CHUNK)

        @pl.when(side == 0)
        def _():
            def body(j, carry):
                q, k, v = [
                    packed[at if i == 0 else pl.ds(0, ROWS), pl.ds(pl.multiple_of(i * HALF + j * 128, 128), 128)]
                    for i in range(3)
                ]
                low = lax.broadcasted_iota(jnp.int32, (ROWS, 128), 1) < 64
                mask = bias[at, :]
                total = head(q, k, v, mask, low, 0.125) + head(q, k, v, mask, jnp.logical_not(low), 0.125)
                mixed[l, h, at, pl.ds(pl.multiple_of(j * 128, 128), 128)] = total.astype(BF)
                return carry

            lax.fori_loop(0, 5, body, 0)

        @pl.when(side == 1)
        def _():
            macc[...] = jnp.zeros((CHUNK, HALF), F32)
            for i in range(8):
                lo, hi = (80 * i) // 128 * 128, (80 * i + 80 + 127) // 128 * 128
                q, k, v = [packed[at if j == 0 else pl.ds(0, ROWS), j * HALF + lo : j * HALF + hi] for j in range(3)]
                lane = lax.broadcasted_iota(jnp.int32, (ROWS, hi - lo), 1) + lo
                keep = (lane >= 80 * i) & (lane < 80 * i + 80)
                macc[:, lo:hi] = macc[:, lo:hi] + head(q, k, v, bias[at, :], keep, 80 ** (-0.5))
            mixed[l, h, at, :] = macc[...].astype(BF)

        piece = mixed.at[l, h, at, :]
        return copies.start(piece, piece, here.partner())

    def out_layer(l, c, copy, to):
        copy.wait_recv()
        at = pl.ds(c * CHUNK, CHUNK)
        update = None
        for b in range(2):
            rows = dot(mixed[l, b, at, :], perm[...]).astype(BF)
            term = dot(rows, flat(wo[l, pl.ds(40 * b, 40), :, :]))
            update = term if update is None else update + term
        x_new = (x_nat[at, :].astype(F32) + update).astype(BF)
        x_nat[at, :] = x_new
        for b in range(2):
            to[b, at, :] = dot(x_nat[at, pl.ds(b * HALF, HALF)], perm[...]).astype(BF)

    def columns(j):
        return pl.ds(pl.multiple_of(j * 512, 512), 512)

    def own_rows(j, carry):
        cols = columns(j)
        rows = dot(enc[side, 0], flat(wp[pl.ds(0, 40), :, cols])) + dot(enc[side, 1], flat(wp[pl.ds(40, 40), :, cols]))
        spread = dot(place[:, pl.ds(pl.multiple_of(side * ROWS, ROWS), ROWS)], rows.astype(BF))
        text[:, cols] = (text[:, cols].astype(F32) + spread).astype(BF)
        return carry

    def other_rows(j, carry):
        cols = columns(j)
        o = 1 - side
        rows = dot(enc[o, 0], flat(wp[pl.ds(0, 40), :, cols])) + dot(enc[o, 1], flat(wp[pl.ds(40, 40), :, cols]))
        spread = dot(place[:, pl.ds(pl.multiple_of(o * ROWS, ROWS), ROWS)], rows.astype(BF))
        out_buf[:, cols] = (text[:, cols].astype(F32) + spread).astype(BF)
        pltpu.make_async_copy(out_buf.at[:, cols], result_ref.at[:, cols], local_sem.at[2 + j]).start()
        return carry

    b0.round(0)
    prepare_perm()
    a0.round(1)
    b0.round(1)
    gp.round(1)
    prepare_rows()
    a0.round(2)
    b0.round(2)
    a1.round(0)
    prepare_bias()
    a0.round(3)
    b0.round(3)
    a1.round(1)
    gp.round(2)
    prepare_place()
    a0.round(4)
    b0.round(4)
    a1.round(2)
    norm(0, 0)
    norm(0, 1)
    a0.round(5)
    b0.round(5)
    a1.round(3)
    gp.round(3)
    a0.round(6)
    a1.round(4)
    a0.round(7)
    project(0)
    b0.round(6)
    b1.round(0)
    m0 = attend(0, 0)
    m1 = attend(0, 1)
    b0.round(7)
    a1.round(5)
    b1.round(1)
    out_layer(0, 0, m0, xp)
    norm(1, 0)
    a1.round(6)
    b1.round(2)
    gp.round(4)
    out_layer(0, 1, m1, xp)
    norm(1, 1)
    a1.round(7)
    project(1)
    b1.round(3)
    m0 = attend(1, 0)
    m1 = attend(1, 1)
    b1.round(4)
    gp.round(5)
    b1.round(5)
    gp.round(6)
    prepare_text()
    b1.round(6)
    b1.round(7)

    def send_across(c):
        piece = enc.at[side, h, pl.ds(c * 64, 64), :]
        return copies.start(piece, piece, here.across())

    def pass_on(c, copy):
        copy.wait_recv()
        piece = enc.at[1 - side, 1 - h, pl.ds(c * 64, 64), :]
        return copies.start(piece, piece, here.partner())

    mine = enc.at[side]
    out_layer(1, 0, m0, mine)
    e0 = [send_across(0), send_across(1)]
    out_layer(1, 1, m1, mine)
    e1 = [send_across(2), send_across(3)]
    gp.round(7)
    f0 = [pass_on(0, e0[0]), pass_on(1, e0[1])]
    lax.fori_loop(0, 1, own_rows, 0)
    f1 = [pass_on(2, e1[0])]
    lax.fori_loop(1, 2, own_rows, 0)
    f1.append(pass_on(3, e1[1]))
    lax.fori_loop(2, 4, own_rows, 0)
    for copy in f0 + f1:
        copy.wait_recv()
    lax.fori_loop(0, 4, other_rows, 0)
    copies.finish()
    for gather in (a0, b0, a1, b1, gp):
        gather.finish()
    assert copies.at[0] <= N_SEND and copies.at[1] <= N_RECV
    for j in range(4):
        cols = pl.ds(j * 512, 512)
        pltpu.make_async_copy(out_buf.at[:, cols], result_ref.at[:, cols], local_sem.at[2 + j]).wait()


def per_device(audio, vision, ids_a, ids_v, order, text, gain, qkv, out_w, proj):
    vm = pl.BlockSpec(memory_space=pltpu.VMEM)
    anywhere = pl.BlockSpec(memory_space=pl.ANY)
    return pl.pallas_call(
        kernel,
        out_shape=jax.ShapeDtypeStruct((768, 2048), BF),
        in_specs=[anywhere, anywhere, vm, vm, vm, anywhere, vm, vm, vm, vm],
        out_specs=anywhere,
        scratch_shapes=[
            pltpu.VMEM((2, 80, 16, 1920), BF),
            pltpu.VMEM((2, 80, 16, 1280), BF),
            pltpu.VMEM((80, 16, 2048), BF),
            pltpu.VMEM((2, 4, 16, 512), BF),
            pltpu.VMEM((2, 4, 16, 384), BF),
            pltpu.VMEM((4, 16, 512), BF),
            pltpu.VMEM((16, 1920), BF),
            pltpu.VMEM((16, 512), BF),
            pltpu.VMEM((2, 16, 1280), BF),
            pltpu.VMEM((2, 16, 1280), BF),
            pltpu.VMEM((ROWS, 1280), BF),
            pltpu.VMEM((2, ROWS, HALF), BF),
            pltpu.VMEM((ROWS, ROWS), F32),
            pltpu.VMEM((HALF, HALF), BF),
            pltpu.VMEM((ROWS, 1280), BF),
            pltpu.VMEM((ROWS, 3 * HALF), BF),
            pltpu.VMEM((CHUNK, HALF), F32),
            pltpu.VMEM((2, 2, ROWS, HALF), BF),
            pltpu.VMEM((2, 2, ROWS, HALF), BF),
            pltpu.VMEM((768, 512), BF),
            pltpu.VMEM((768, 2048), BF),
            pltpu.VMEM((768, 2048), BF),
            pltpu.SemaphoreType.DMA((N_SEND,)),
            pltpu.SemaphoreType.DMA((N_RECV,)),
            pltpu.SemaphoreType.DMA((8,)),
        ],
        name="encode",
        compiler_params=pltpu.CompilerParams(collective_id=0, has_side_effects=True, vmem_limit_bytes=56 * 2**20),
        cost_estimate=pl.CostEstimate(flops=12_000_000_000, bytes_accessed=30_000_000, transcendentals=2_000_000),
    )(audio, vision, ids_a, ids_v, order, text, gain, qkv, out_w, proj)


def solution(mesh):
    placed = (
        P(("dp", "fsdp"), None),
        P(("dp", "fsdp"), None),
        P(("dp", "fsdp"), None),
        P(("dp", "fsdp"), None),
        P(("dp", "fsdp"), None),
        P(("dp", "fsdp"), "phase"),
        P("phase", None),
        P("phase", ("dp", "fsdp"), None),
        P("phase", ("dp", "fsdp"), None),
        P(("dp", "fsdp"), "phase"),
    )
    return jax.shard_map(
        per_device,
        mesh=mesh,
        in_specs=placed,
        out_specs=P(("dp", "fsdp"), "phase"),
        check_vma=False,
    )
```
